32 devices in a mesh: date: 8 (over z, core), path: 4 (over y, x).
Axes of the slice: x: 2, y: 2, z: 4, core: 2. Of those that a mesh axis runs over, the one named last changes fastest.
Arguments:
- features: bfloat16 [16, 512, 2048], P('date', 'path'), may hold values from -6 to 6
- payoff: float32 [16, 512, 256], P('date', 'path'), may hold values from -8 to 64
- coefficients: bfloat16 [2048, 256], replicated, may hold values from -0.02734375 to 0.02734375
- exercise: int32 [16, 256], P('date'), may hold values from 0 to 1, as said below
Outputs:
- gradient: float32 [2048, 256], P(('date', 'path'))
- bound: float32 [256], replicated
- spread: float32 [256], replicated
The draws below stay inside these ranges and needn't reach their ends.
Inputs may be any that keep to these rules, and one draw needn't show every extreme that they name: `exercise`: every contract may be exercised at the first and at the last date.
All inputs are finite; a program needn't handle non-finite values.
Results may differ from the reference program's by a relative error of at most 0.0017.
Values sent between devices are 32-bit elements; how exact they have to be, the bound alone decides.
No kernel may reach another device: no remote copies, remote signals or barrier semaphores. Data moves between devices by JAX's collectives and lax.ppermute only.
A program may use at most 64 MiB of HBM per device.

```python
import jax
import jax.numpy as jnp

K = 2048
C = 256
DATES = 16
PATHS = 512


def draw_payoff(key, part):
    first = jax.random.fold_in(key, 0)
    return jax.random.normal(first, (DATES, PATHS, C), jnp.float32)


def draw_exercise(key, part):
    levels = jax.random.randint(jax.random.fold_in(key, 7), (DATES, C), 0, 4)
    dates = jnp.arange(DATES)[:, None]
    edges = (dates == 0) | (dates == DATES - 1)
    return jnp.where(edges | (levels > 0), 1, 0).astype(jnp.int32)


def spiked(drawn, key, source, target, blocks, factor):
    def block_of(axis_at):
        return (jnp.arange(drawn.shape[axis_at]) // (drawn.shape[axis_at] // blocks)).reshape((-1,) + (1,) * (drawn.ndim - 1 - axis_at))

    first = jax.random.permutation(key, blocks)[block_of(target)]
    second = (block_of(target) + blocks // 2) % blocks
    return jnp.where((block_of(source) == first) | (block_of(source) == second), factor * drawn, drawn)


def block_levels(own_key, shape, pieces, low, high):
    def one(position, blocks):
        steps = jax.random.uniform(jax.random.fold_in(jax.random.fold_in(own_key, 6), position), (blocks,), jnp.float32, low / len(pieces), high / len(pieces))
        return jnp.repeat(jnp.exp(steps), shape[position] // blocks).reshape((-1,) + (1,) * (len(shape) - position - 1))

    level = one(*pieces[0])
    for cut in pieces[1:]:
        level = level * one(*cut)
    return level


def centred(rng, shape, scale, most, cuts=(), kind=jnp.bfloat16):
    loudness = block_levels(rng, shape, cuts, -0.22, 0.18) if cuts else 1.0
    result = jax.random.normal(rng, shape, jnp.float32) * scale * loudness
    return jnp.minimum(jnp.maximum(result, -most), most).astype(kind)


def bell_draw_with(own_key, extent, deviation, reach, pieces, heavy, dtype=jnp.bfloat16):
    entries = deviation * jax.random.normal(own_key, extent, jnp.float32)
    if pieces:
        entries = entries * block_levels(own_key, extent, pieces, -0.22, 0.18)
    return jnp.clip(spiked(entries, jax.random.fold_in(own_key, 3), *heavy), -reach, reach).astype(dtype)


def setup_inputs(seed: int = 0) -> dict:
    seeds = jax.random.split(jax.random.key(seed), 5)
    features = bell_draw_with(seeds[0], (DATES, PATHS, K), 1.0, 6.0, ((0, 8), (1, 4)), (1, 2, 4, 2.0))
    payoff = draw_payoff(jax.random.fold_in(seeds[4], 71), 0)
    coefficients = centred(seeds[2], (K, C), (25 * K) ** -0.5, 0.02734375)
    exercise = draw_exercise(jax.random.fold_in(seeds[4], 71), 0)
    return dict(features=features, payoff=payoff, coefficients=coefficients, exercise=exercise)


TEMP = 0.25
NEG = -1e30


def reference(features, payoff, coefficients, exercise):
    flat = features.reshape(-1, K)
    increments = jnp.dot(flat, coefficients, preferred_element_type=jnp.float32).reshape(DATES, PATHS, C)
    martingale = jnp.cumsum(increments, axis=0)
    allowed = exercise[:, None, :] > 0
    score = jnp.where(allowed, (payoff - martingale) / TEMP, NEG)
    peak = jnp.max(score, axis=0)
    shifted = jnp.exp(score - peak[None])
    total = jnp.sum(shifted, axis=0)
    smoothed = TEMP * (peak + jnp.log(total))
    weight = shifted / total[None]
    tail = jnp.flip(jnp.cumsum(jnp.flip(weight, 0), axis=0), 0).astype(jnp.bfloat16)
    gradient = -jnp.dot(flat.T, tail.reshape(-1, C), preferred_element_type=jnp.float32) / PATHS
    bound = jnp.sum(smoothed, axis=0) / PATHS
    spread = jnp.sum(smoothed * smoothed, axis=0) / PATHS - bound * bound
    return gradient, bound, spread
```

```python
import functools

import jax
import jax.numpy as jnp
from jax import lax
from jax.experimental import pallas as pl
from jax.experimental.pallas import tpu as pltpu
from jax.sharding import PartitionSpec as P

INVERSE_TEMP = 4.0
TEMP = 0.25
NEG = -1e30
STAT_ROWS = 8
VMEM_LIMIT = 16 << 20
f32 = jnp.float32
bf16 = jnp.bfloat16


def core_of():
    return lax.axis_index("date") % 2


def chip_of():
    return lax.axis_index("date") // 2


def call(body, outs, *operands, scratch=(), flops=0, unread=0):
    whole = pl.BlockSpec(memory_space=pltpu.VMEM)
    anywhere = pl.BlockSpec(memory_space=pl.ANY)
    read = len(operands) - unread

    def kernel(*refs):
        body(*refs[:read], *refs[read + unread :])

    return pl.pallas_call(
        kernel,
        out_shape=[jax.ShapeDtypeStruct(*o) for o in outs],
        in_specs=[whole] * read + [anywhere] * unread,
        out_specs=[whole] * len(outs),
        scratch_shapes=list(scratch),
        compiler_params=pltpu.CompilerParams(vmem_limit_bytes=VMEM_LIMIT),
        cost_estimate=pl.CostEstimate(flops=flops, bytes_accessed=0, transcendentals=0),
    )(*operands)


def log_add(a, b):
    return jnp.maximum(a, b) + jnp.log(1.0 + jnp.exp(-jnp.abs(a - b)))


def increments_body(features, coefficients, payoff, exercise, keep, send, inc):
    dates, paths, width = features.shape
    half = paths // 2
    product = jnp.dot(features[...].reshape(dates * paths, width), coefficients[...], preferred_element_type=f32)
    inc[...] = (INVERSE_TEMP * product).reshape(inc.shape)
    mine = pl.multiple_of(core_of() * half, half)
    theirs = pl.multiple_of((1 - core_of()) * half, half)
    for out, at in ((keep, mine), (send, theirs)):
        out[0:dates] = inc[:, pl.ds(at, half)]
        for d in range(dates):
            allowed = exercise[d : d + 1, :] > 0
            out[dates + d] = jnp.where(allowed, INVERSE_TEMP * payoff[d, pl.ds(at, half)], NEG)


def message_of(level, total, left, last):
    if last:
        return [jnp.where(left, level + total, level)]
    return [level, total]


def local_body(rounds, keep, other, score, level, total, message):
    dates = keep.shape[0] // 2
    first = core_of() == 0
    run = jnp.zeros(keep.shape[1:], f32)
    scores = []
    for part in (0, 1):
        for d in range(dates):
            inc, base = (
                jnp.where(first == (part == 0), keep[at], other[at]) for at in (d, dates + d)
            )
            run = run + inc
            scores.append(base - run)
    peak = functools.reduce(jnp.maximum, scores)
    lev = peak + jnp.log(sum(jnp.exp(s - peak) for s in scores))
    for i, s in enumerate(scores):
        score[i] = s
    level[...] = lev
    total[...] = run
    left = chip_of() % 2 == 0
    for i, m in enumerate(message_of(lev, run, left, rounds == 1)):
        message[i] = m


def merge_body(step, rounds, level, total, state, got, level2, total2, state2, message):
    left = (chip_of() >> step) % 2 == 0
    lev, tot, other_lev, other_tot = level[...], total[...], got[0], got[1]
    if state is None:
        zero = jnp.zeros_like(lev)
        before, after, sum_before, sum_after = zero + NEG, zero + NEG, zero, zero
    else:
        before, after, sum_before, sum_after = (state[i] for i in range(4))
    state2[0] = jnp.where(left, before, log_add(before, other_lev + other_tot + sum_before))
    state2[1] = jnp.where(left, log_add(after, other_lev - sum_after), after)
    state2[2] = jnp.where(left, sum_before, sum_before + other_tot)
    state2[3] = jnp.where(left, sum_after + other_tot, sum_after)
    first_lev, first_tot = jnp.where(left, lev, other_lev), jnp.where(left, tot, other_tot)
    second_lev = jnp.where(left, other_lev, lev)
    lev2 = log_add(first_lev, second_lev - first_tot)
    tot2 = tot + other_tot
    level2[...] = lev2
    total2[...] = tot2
    next_left = (chip_of() >> (step + 1)) % 2 == 0
    for i, m in enumerate(message_of(lev2, tot2, next_left, step + 2 == rounds)):
        message[i] = m


def tail_body(rounds, score, level, total, state, got, out):
    lev, tot = level[...], total[...]
    zero = jnp.zeros_like(lev)
    if state is None:
        before, after, sum_before, sum_after = zero + NEG, zero + NEG, zero, zero
    else:
        before, after, sum_before, sum_after = (state[i] for i in range(4))
    if got is not None:
        left = (chip_of() >> (rounds - 1)) % 2 == 0
        other = got[0]
        before = jnp.where(left, before, log_add(before, other + sum_before))
        after = jnp.where(left, log_add(after, other - sum_after), after)
    later = after - tot
    norm = log_add(log_add(before, lev), later)
    run = jnp.exp(later - norm)
    half = score.shape[1]
    for i in reversed(range(score.shape[0])):
        run = run + jnp.exp(score[i] - norm)
        out[i * half : (i + 1) * half, :] = run.astype(bf16).astype(f32)
    smoothed = jnp.where(chip_of() == 0, TEMP * norm, 0.0)
    at = score.shape[0] * half
    out[at : at + STAT_ROWS, :] = jnp.zeros((STAT_ROWS, smoothed.shape[1]), f32)
    out[at : at + 1, :] = jnp.sum(smoothed, axis=0, keepdims=True)
    out[at + 1 : at + 2, :] = jnp.sum(smoothed * smoothed, axis=0, keepdims=True)


def halves_body(chips, features, send):
    width = features.shape[2] // (2 * chips)
    for z in range(chips):
        at = pl.multiple_of((2 * z + 1 - core_of()) * width, width)
        send[:, :, z * width : (z + 1) * width] = features[:, :, pl.ds(at, width)].astype(f32)


def columns_body(chips, features, got, columns):
    dates, paths, whole = features.shape
    width = whole // (2 * chips)
    mine, theirs = core_of() * dates, (1 - core_of()) * dates
    for z in range(chips):
        at = pl.multiple_of((2 * z + core_of()) * width, width)
        rows = slice(z * width, (z + 1) * width)
        for d in range(dates):
            own = features[d, :, pl.ds(at, width)].T
            columns[rows, pl.ds(pl.multiple_of((mine + d) * paths, paths), paths)] = own
            other = got[d, :, rows].astype(bf16).T
            columns[rows, pl.ds(pl.multiple_of((theirs + d) * paths, paths), paths)] = other


def product_body(scale, paths_count, columns, own, got, keep, *rest):
    messages, (tail, product) = rest[: paths_count - 1], rest[paths_count - 1 :]
    dates, paths, contracts = tail.shape
    half = paths // 2
    for source, at in ((own, core_of()), (got, 1 - core_of())):
        rows = pl.ds(pl.multiple_of(at * half, half), half)
        for d in range(dates):
            tail[d, rows] = source[d * half : (d + 1) * half, :].astype(bf16)
    right = tail[...].reshape(dates * paths, contracts)
    chips, count, rows, _ = product.shape
    width = count * rows
    for z in range(chips):
        block = jnp.dot(columns[z * width : (z + 1) * width, :], right, preferred_element_type=f32)
        product[z] = (scale * block).reshape(count, rows, contracts)
    stats = own[dates * half :, :] + got[dates * half :, :]
    me = lax.axis_index("path")
    for j, out in enumerate((keep, *messages)):
        for z in range(chips):
            out[z * rows : (z + 1) * rows, :] = product[z, partner(me, j, count)]
        out[chips * rows :, :] = stats


def partner(me, j, count):
    if count & (count - 1) == 0:
        return me ^ j
    return lax.rem(me + j, count)


def pairs(count, j):
    if count & (count - 1) == 0:
        return [(i, i ^ j) for i in range(count)]
    return [(i, (i + j) % count) for i in range(count)]


def date_pairs(chips, j):
    return [(2 * a + core, 2 * b + core) for a, b in pairs(chips, j) for core in range(2)]


def path_sum_body(count, chips, *refs):
    parts, (keep, *messages), (total,) = refs[:count], refs[count : count + chips], refs[count + chips :]
    total[...] = functools.reduce(lambda a, b: a + b, (p[...] for p in parts))
    rows = (total.shape[0] - STAT_ROWS) // chips
    for j, out in enumerate((keep, *messages)):
        at = pl.multiple_of(partner(chip_of(), j, chips) * rows, rows)
        out[0:rows, :] = total[pl.ds(at, rows), :]
        out[rows:, :] = total[chips * rows :, :]


def date_sum_body(chips, paths_total, *refs):
    parts, (gradient, bound, spread) = refs[:chips], refs[chips:]
    total = functools.reduce(lambda a, b: a + b, (p[...] for p in parts))
    rows = gradient.shape[0]
    gradient[...] = total[:rows, :]
    mean = total[rows : rows + 1, :] * (1.0 / paths_total)
    bound[...] = mean
    spread[...] = total[rows + 1 : rows + 2, :] * (1.0 / paths_total) - mean * mean


def shards(features, payoff, coefficients, exercise):
    dates, paths, width = features.shape
    contracts = coefficients.shape[1]
    chips, count = lax.axis_size("date") // 2, lax.axis_size("path")
    rounds = chips.bit_length() - 1
    assert chips == 1 << rounds
    half, paths_total = paths // 2, paths * count
    rows = width // (2 * chips * count)
    cores = [(2 * z + c, 2 * z + 1 - c) for z in range(chips) for c in range(2)]
    plane = (half, contracts)

    keep, send = call(
        increments_body,
        [((2 * dates, *plane), f32)] * 2,
        features,
        coefficients,
        payoff,
        exercise,
        scratch=[pltpu.VMEM((dates, paths, contracts), f32)],
        flops=2 * dates * paths * width * contracts,
    )
    other = lax.ppermute(send, "date", cores)
    sizes = [1 if step + 1 == rounds else 2 for step in range(rounds)] or [2]
    score, level, total, message = call(
        functools.partial(local_body, rounds),
        [((2 * dates, *plane), f32), (plane, f32), (plane, f32), ((sizes[0], *plane), f32)],
        keep,
        other,
    )
    (columns_send,) = call(
        functools.partial(halves_body, chips),
        [((dates, paths, width // 2), f32)],
        features,
        message,
        unread=1,
        flops=1 << 26,
    )
    own_level, own_total, state, got = level, total, None, None
    columns_got = lax.ppermute(columns_send, "date", cores)
    for step in range(rounds):
        got = lax.ppermute(message, "date", date_pairs(chips, 1 << step))
        if step + 1 == rounds:
            break
        body = functools.partial(merge_body, step, rounds)
        if state is None:
            body = lambda a, b, c, *o, body=body: body(a, b, None, c, *o)
        operands = [level, total, got] if state is None else [level, total, state, got]
        level, total, state, message = call(
            body,
            [(plane, f32), (plane, f32), ((4, *plane), f32), ((sizes[step + 1], *plane), f32)],
            *operands,
        )
    (columns,) = call(
        functools.partial(columns_body, chips),
        [((width // 2, 2 * dates * paths), bf16)],
        features,
        columns_got,
        message,
        unread=1,
        flops=1 << 27,
    )
    extra = [x for x in (state, got) if x is not None]

    def tail_kernel(score, level, total, *rest):
        rest = list(rest)
        given = rest.pop(0) if state is not None else None
        arrived = rest.pop(0) if got is not None else None
        tail_body(rounds, score, level, total, given, arrived, *rest)

    (tail,) = call(
        tail_kernel,
        [((2 * dates * half + STAT_ROWS, contracts), f32)],
        score,
        own_level,
        own_total,
        *extra,
    )
    tail_other = lax.ppermute(tail, "date", cores)
    partial_shape = ((chips * rows + STAT_ROWS, contracts), f32)
    pieces = call(
        functools.partial(product_body, -1.0 / paths_total, count),
        [partial_shape] * count,
        columns,
        tail,
        tail_other,
        scratch=[
            pltpu.VMEM((2 * dates, paths, contracts), bf16),
            pltpu.VMEM((chips, count, rows, contracts), f32),
        ],
        flops=2 * dates * paths * width * contracts,
    )
    pieces = [pieces[0]] + [lax.ppermute(m, "path", pairs(count, j)) for j, m in enumerate(pieces) if j]
    pieces = call(
        functools.partial(path_sum_body, count, chips),
        [((rows + STAT_ROWS, contracts), f32)] * chips,
        *pieces,
        scratch=[pltpu.VMEM(*partial_shape)],
    )
    pieces = [pieces[0]] + [lax.ppermute(m, "date", date_pairs(chips, j)) for j, m in enumerate(pieces) if j]
    gradient, bound, spread = call(
        functools.partial(date_sum_body, chips, paths_total),
        [((rows, contracts), f32), ((1, contracts), f32), ((1, contracts), f32)],
        *pieces,
    )
    return gradient, bound.reshape(contracts), spread.reshape(contracts)


def solution(mesh):
    placed = (P("date", "path", None), P("date", "path", None), P(), P("date", None))
    return jax.shard_map(
        shards,
        mesh=mesh,
        in_specs=placed,
        out_specs=(P(("date", "path"), None), P(), P()),
        check_vma=False,
    )
```

```python
import functools

import jax
import jax.numpy as jnp
from jax import lax
from jax.experimental import pallas as pl
from jax.experimental.pallas import tpu as pltpu
from jax.sharding import PartitionSpec as P

INVERSE_TEMP = 4.0
TEMP = 0.25
NEG = -1e30
STAT_ROWS = 8
PIECES = 4
VMEM_LIMIT = 16 << 20
f32 = jnp.float32
bf16 = jnp.bfloat16


def core_of():
    return lax.axis_index("date") % 2


def chip_of():
    return lax.axis_index("date") // 2


def call(body, outs, *operands, scratch=(), flops=0, unread=0, place=pltpu.VMEM):
    given, whole = pl.BlockSpec(memory_space=place), pl.BlockSpec(memory_space=pltpu.VMEM)
    anywhere = pl.BlockSpec(memory_space=pl.ANY)
    read = len(operands) - unread
    if place is pltpu.HBM:
        operands = [pltpu.with_memory_space_constraint(x, place) for x in operands]

    def kernel(*refs):
        body(*refs[:read], *refs[read + unread :])

    return pl.pallas_call(
        kernel,
        out_shape=[jax.ShapeDtypeStruct(*o) for o in outs],
        in_specs=[given] * read + [anywhere] * unread,
        out_specs=[whole] * len(outs),
        scratch_shapes=list(scratch),
        compiler_params=pltpu.CompilerParams(vmem_limit_bytes=VMEM_LIMIT),
        cost_estimate=pl.CostEstimate(flops=flops, bytes_accessed=0, transcendentals=0),
    )(*operands)


def log_add(a, b):
    return jnp.maximum(a, b) + jnp.log(1.0 + jnp.exp(-jnp.abs(a - b)))


def increments_body(features, coefficients, payoff, exercise, keep, send, held, inc, weights, pay, may, sems):
    dates, paths, width = features.shape
    half, step = paths // 2, width // PIECES
    copies = []
    for i in range(PIECES):
        at = slice(i * step, (i + 1) * step)
        copies.append(pltpu.make_async_copy(features.at[:, :, at], held.at[:, :, at], sems.at[2 * i]))
        copies.append(pltpu.make_async_copy(coefficients.at[at, :], weights.at[at, :], sems.at[2 * i + 1]))
    copies.append(pltpu.make_async_copy(payoff, pay, sems.at[2 * PIECES]))
    copies.append(pltpu.make_async_copy(exercise, may, sems.at[2 * PIECES + 1]))
    for c in copies:
        c.start()
    for i in range(PIECES):
        at = slice(i * step, (i + 1) * step)
        copies[2 * i].wait()
        copies[2 * i + 1].wait()
        left = held[:, :, at].reshape(dates * paths, step)
        part = jnp.dot(left, weights[at, :], preferred_element_type=f32).reshape(inc.shape)
        inc[...] = part if i == 0 else inc[...] + part
    copies[-2].wait()
    copies[-1].wait()
    mine = pl.multiple_of(core_of() * half, half)
    theirs = pl.multiple_of((1 - core_of()) * half, half)
    for out, at in ((keep, mine), (send, theirs)):
        out[0:dates] = INVERSE_TEMP * inc[:, pl.ds(at, half)]
        for d in range(dates):
            allowed = may[d : d + 1, :] > 0
            out[dates + d] = jnp.where(allowed, INVERSE_TEMP * pay[d, pl.ds(at, half)], NEG)


def message_of(level, total, left, last):
    if last:
        return [jnp.where(left, level + total, level)]
    return [level, total]


def local_body(rounds, keep, other, score, level, total, message):
    dates = keep.shape[0] // 2
    first = core_of() == 0
    run = jnp.zeros(keep.shape[1:], f32)
    scores = []
    for part in (0, 1):
        for d in range(dates):
            inc, base = (
                jnp.where(first == (part == 0), keep[at], other[at]) for at in (d, dates + d)
            )
            run = run + inc
            scores.append(base - run)
    peak = functools.reduce(jnp.maximum, scores)
    lev = peak + jnp.log(sum(jnp.exp(s - peak) for s in scores))
    for i, s in enumerate(scores):
        score[i] = s
    level[...] = lev
    total[...] = run
    left = chip_of() % 2 == 0
    for i, m in enumerate(message_of(lev, run, left, rounds == 1)):
        message[i] = m


def merge_body(step, rounds, level, total, state, got, state2, message, *group):
    left = (chip_of() >> step) % 2 == 0
    lev, tot, other_lev, other_tot = level[...], total[...], got[0], got[1]
    if state is None:
        zero = jnp.zeros_like(lev)
        before, after, sum_before, sum_after = zero + NEG, zero + NEG, zero, zero
    else:
        before, after, sum_before, sum_after = (state[i] for i in range(4))
    state2[0] = jnp.where(left, before, log_add(before, other_lev + other_tot + sum_before))
    state2[1] = jnp.where(left, log_add(after, other_lev - sum_after), after)
    state2[2] = jnp.where(left, sum_before, sum_before + other_tot)
    state2[3] = jnp.where(left, sum_after + other_tot, sum_after)
    first_lev, first_tot = jnp.where(left, lev, other_lev), jnp.where(left, tot, other_tot)
    second_lev = jnp.where(left, other_lev, lev)
    lev2 = log_add(first_lev, second_lev - first_tot)
    tot2 = tot + other_tot
    for out, value in zip(group, (lev2, tot2)):
        out[...] = value
    next_left = (chip_of() >> (step + 1)) % 2 == 0
    for i, m in enumerate(message_of(lev2, tot2, next_left, step + 2 == rounds)):
        message[i] = m


def tail_body(rounds, score, level, total, state, got, out):
    lev, tot = level[...], total[...]
    zero = jnp.zeros_like(lev)
    if state is None:
        before, after, sum_before, sum_after = zero + NEG, zero + NEG, zero, zero
    else:
        before, after, sum_before, sum_after = (state[i] for i in range(4))
    if got is not None:
        left = (chip_of() >> (rounds - 1)) % 2 == 0
        other = got[0]
        before = jnp.where(left, before, log_add(before, other + sum_before))
        after = jnp.where(left, log_add(after, other - sum_after), after)
    later = after - tot
    norm = log_add(log_add(before, lev), later)
    run = jnp.exp(later - norm)
    half = score.shape[1]
    for i in reversed(range(score.shape[0])):
        run = run + jnp.exp(score[i] - norm)
        out[i * half : (i + 1) * half, :] = run.astype(bf16).astype(f32)
    smoothed = jnp.where(chip_of() == 0, TEMP * norm, 0.0)
    at = score.shape[0] * half
    out[at : at + STAT_ROWS, :] = jnp.zeros((STAT_ROWS, smoothed.shape[1]), f32)
    out[at : at + 1, :] = jnp.sum(smoothed, axis=0, keepdims=True)
    out[at + 1 : at + 2, :] = jnp.sum(smoothed * smoothed, axis=0, keepdims=True)


def halves_body(chips, features, send):
    width = features.shape[2] // (2 * chips)
    for z in range(chips):
        at = pl.multiple_of((2 * z + 1 - core_of()) * width, width)
        send[:, :, z * width : (z + 1) * width] = features[:, :, pl.ds(at, width)].astype(f32)


def columns_body(chips, features, got, columns):
    dates, paths, whole = features.shape
    width = whole // (2 * chips)
    mine, theirs = core_of() * dates, (1 - core_of()) * dates
    for z in range(chips):
        at = pl.multiple_of((2 * z + core_of()) * width, width)
        rows = slice(z * width, (z + 1) * width)
        for d in range(dates):
            own = features[d, :, pl.ds(at, width)].T
            columns[rows, pl.ds(pl.multiple_of((mine + d) * paths, paths), paths)] = own
            other = got[d, :, rows].astype(bf16).T
            columns[rows, pl.ds(pl.multiple_of((theirs + d) * paths, paths), paths)] = other


def product_body(scale, paths_count, columns, own, got, keep, *rest):
    messages, (tail, product) = rest[: paths_count - 1], rest[paths_count - 1 :]
    dates, paths, contracts = tail.shape
    half = paths // 2
    for source, at in ((own, core_of()), (got, 1 - core_of())):
        rows = pl.ds(pl.multiple_of(at * half, half), half)
        for d in range(dates):
            tail[d, rows] = source[d * half : (d + 1) * half, :].astype(bf16)
    right = tail[...].reshape(dates * paths, contracts)
    chips, count, rows, _ = product.shape
    width = count * rows
    for z in range(chips):
        block = jnp.dot(columns[z * width : (z + 1) * width, :], right, preferred_element_type=f32)
        product[z] = (scale * block).reshape(count, rows, contracts)
    stats = own[dates * half :, :] + got[dates * half :, :]
    me = lax.axis_index("path")
    for j, out in enumerate((keep, *messages)):
        for z in range(chips):
            out[z * rows : (z + 1) * rows, :] = product[z, partner(me, j, count)]
        out[chips * rows :, :] = stats


def partner(me, j, count):
    if count & (count - 1) == 0:
        return me ^ j
    return lax.rem(me + j, count)


def pairs(count, j):
    if count & (count - 1) == 0:
        return [(i, i ^ j) for i in range(count)]
    return [(i, (i + j) % count) for i in range(count)]


def date_pairs(chips, j):
    return [(2 * a + core, 2 * b + core) for a, b in pairs(chips, j) for core in range(2)]


def path_sum_body(count, chips, *refs):
    parts, (keep, *messages), (total,) = refs[:count], refs[count : count + chips], refs[count + chips :]
    total[...] = functools.reduce(lambda a, b: a + b, (p[...] for p in parts))
    rows = (total.shape[0] - STAT_ROWS) // chips
    for j, out in enumerate((keep, *messages)):
        at = pl.multiple_of(partner(chip_of(), j, chips) * rows, rows)
        out[0:rows, :] = total[pl.ds(at, rows), :]
        out[rows:, :] = total[chips * rows :, :]


def date_sum_body(chips, paths_total, *refs):
    parts, (gradient, bound, spread) = refs[:chips], refs[chips:]
    total = functools.reduce(lambda a, b: a + b, (p[...] for p in parts))
    rows = gradient.shape[0]
    gradient[...] = total[:rows, :]
    mean = total[rows : rows + 1, :] * (1.0 / paths_total)
    bound[...] = mean
    spread[...] = total[rows + 1 : rows + 2, :] * (1.0 / paths_total) - mean * mean


def shards(features, payoff, coefficients, exercise):
    dates, paths, width = features.shape
    contracts = coefficients.shape[1]
    chips, count = lax.axis_size("date") // 2, lax.axis_size("path")
    rounds = chips.bit_length() - 1
    assert chips == 1 << rounds
    half, paths_total = paths // 2, paths * count
    rows = width // (2 * chips * count)
    cores = [(2 * z + c, 2 * z + 1 - c) for z in range(chips) for c in range(2)]
    plane = (half, contracts)

    keep, send, held = call(
        increments_body,
        [((2 * dates, *plane), f32), ((2 * dates, *plane), f32), (features.shape, bf16)],
        features,
        coefficients,
        payoff,
        exercise,
        scratch=[
            pltpu.VMEM((dates, paths, contracts), f32),
            pltpu.VMEM(coefficients.shape, bf16),
            pltpu.VMEM(payoff.shape, f32),
            pltpu.VMEM(exercise.shape, jnp.int32),
            pltpu.SemaphoreType.DMA((2 * PIECES + 2,)),
        ],
        flops=2 * dates * paths * width * contracts,
        place=pltpu.HBM,
    )
    other = lax.ppermute(send, "date", cores)
    sizes = [1 if step + 1 == rounds else 2 for step in range(rounds)] or [2]
    score, level, total, message = call(
        functools.partial(local_body, rounds),
        [((2 * dates, *plane), f32), (plane, f32), (plane, f32), ((sizes[0], *plane), f32)],
        keep,
        other,
    )
    (columns_send,) = call(
        functools.partial(halves_body, chips),
        [((dates, paths, width // 2), f32)],
        held,
        message,
        unread=1,
        flops=1 << 26,
    )
    own_level, own_total, state, got = level, total, None, None
    columns_got = lax.ppermute(columns_send, "date", cores)
    for step in range(rounds):
        got = lax.ppermute(message, "date", date_pairs(chips, 1 << step))
        if step + 1 == rounds:
            break
        body = functools.partial(merge_body, step, rounds)
        if state is None:
            body = lambda a, b, c, *o, body=body: body(a, b, None, c, *o)
        operands = [level, total, got] if state is None else [level, total, state, got]
        group = [(plane, f32)] * (0 if step + 2 == rounds else 2)
        state, message, *group = call(body, [((4, *plane), f32), ((sizes[step + 1], *plane), f32)] + group, *operands)
        level, total = group or (level, total)
    (columns,) = call(
        functools.partial(columns_body, chips),
        [((width // 2, 2 * dates * paths), bf16)],
        held,
        columns_got,
        message,
        unread=1,
        flops=1 << 27,
    )
    extra = [x for x in (state, got) if x is not None]

    def tail_kernel(score, level, total, *rest):
        rest = list(rest)
        given = rest.pop(0) if state is not None else None
        arrived = rest.pop(0) if got is not None else None
        tail_body(rounds, score, level, total, given, arrived, *rest)

    (tail,) = call(
        tail_kernel,
        [((2 * dates * half + STAT_ROWS, contracts), f32)],
        score,
        own_level,
        own_total,
        *extra,
    )
    tail_other = lax.ppermute(tail, "date", cores)
    partial_shape = ((chips * rows + STAT_ROWS, contracts), f32)
    pieces = call(
        functools.partial(product_body, -1.0 / paths_total, count),
        [partial_shape] * count,
        columns,
        tail,
        tail_other,
        scratch=[
            pltpu.VMEM((2 * dates, paths, contracts), bf16),
            pltpu.VMEM((chips, count, rows, contracts), f32),
        ],
        flops=2 * dates * paths * width * contracts,
    )
    pieces = [pieces[0]] + [lax.ppermute(m, "path", pairs(count, j)) for j, m in enumerate(pieces) if j]
    pieces = call(
        functools.partial(path_sum_body, count, chips),
        [((rows + STAT_ROWS, contracts), f32)] * chips,
        *pieces,
        scratch=[pltpu.VMEM(*partial_shape)],
    )
    pieces = [pieces[0]] + [lax.ppermute(m, "date", date_pairs(chips, j)) for j, m in enumerate(pieces) if j]
    gradient, bound, spread = call(
        functools.partial(date_sum_body, chips, paths_total),
        [((rows, contracts), f32), ((1, contracts), f32), ((1, contracts), f32)],
        *pieces,
    )
    return gradient, bound.reshape(contracts), spread.reshape(contracts)


def solution(mesh):
    placed = (P("date", "path", None), P("date", "path", None), P(), P("date", None))
    return jax.shard_map(
        shards,
        mesh=mesh,
        in_specs=placed,
        out_specs=(P(("date", "path"), None), P(), P()),
        check_vma=False,
    )
```

```python
import functools

import jax
import jax.numpy as jnp
from jax import lax
from jax.experimental import pallas as pl
from jax.experimental.pallas import tpu as pltpu
from jax.sharding import PartitionSpec as P

INVERSE_TEMP = 4.0
TEMP = 0.25
NEG = -1e30
STAT_ROWS = 8
PIECES = 4
VMEM_LIMIT = 16 << 20
f32 = jnp.float32
bf16 = jnp.bfloat16


def core_of():
    return lax.axis_index("date") % 2


def chip_of():
    return lax.axis_index("date") // 2


def call(body, outs, *operands, scratch=(), flops=0, unread=0, place=pltpu.VMEM):
    given, whole = pl.BlockSpec(memory_space=place), pl.BlockSpec(memory_space=pltpu.VMEM)
    anywhere = pl.BlockSpec(memory_space=pl.ANY)
    read = len(operands) - unread
    if place is pltpu.HBM:
        operands = [pltpu.with_memory_space_constraint(x, place) for x in operands]

    def kernel(*refs):
        body(*refs[:read], *refs[read + unread :])

    return pl.pallas_call(
        kernel,
        out_shape=[jax.ShapeDtypeStruct(*o) for o in outs],
        in_specs=[given] * read + [anywhere] * unread,
        out_specs=[whole] * len(outs),
        scratch_shapes=list(scratch),
        compiler_params=pltpu.CompilerParams(vmem_limit_bytes=VMEM_LIMIT),
        cost_estimate=pl.CostEstimate(flops=flops, bytes_accessed=0, transcendentals=0),
    )(*operands)


def log_add(a, b):
    return jnp.maximum(a, b) + jnp.log(1.0 + jnp.exp(-jnp.abs(a - b)))


def increments_body(features, coefficients, payoff, exercise, keep, send, held, inc, weights, pay, may, sems):
    dates, paths, width = features.shape
    half, step = paths // 2, width // PIECES
    copies = []
    for i in range(PIECES):
        at = slice(i * step, (i + 1) * step)
        copies.append(pltpu.make_async_copy(features.at[:, :, at], held.at[:, :, at], sems.at[2 * i]))
        copies.append(pltpu.make_async_copy(coefficients.at[at, :], weights.at[at, :], sems.at[2 * i + 1]))
    copies.append(pltpu.make_async_copy(payoff, pay, sems.at[2 * PIECES]))
    copies.append(pltpu.make_async_copy(exercise, may, sems.at[2 * PIECES + 1]))
    for c in copies:
        c.start()
    for i in range(PIECES):
        at = slice(i * step, (i + 1) * step)
        copies[2 * i].wait()
        copies[2 * i + 1].wait()
        left = held[:, :, at].reshape(dates * paths, step)
        part = jnp.dot(left, weights[at, :], preferred_element_type=f32).reshape(inc.shape)
        inc[...] = part if i == 0 else inc[...] + part
    copies[-2].wait()
    copies[-1].wait()
    mine = pl.multiple_of(core_of() * half, half)
    theirs = pl.multiple_of((1 - core_of()) * half, half)
    for out, at in ((keep, mine), (send, theirs)):
        out[0:dates] = INVERSE_TEMP * inc[:, pl.ds(at, half)]
        for d in range(dates):
            allowed = may[d : d + 1, :] > 0
            out[dates + d] = jnp.where(allowed, INVERSE_TEMP * pay[d, pl.ds(at, half)], NEG)


def message_of(level, total, left, last):
    if last:
        return [jnp.where(left, level + total, level)]
    return [level, total]


def local_body(rounds, keep, other, score, level, total, message):
    dates = keep.shape[0] // 2
    first = core_of() == 0
    run = jnp.zeros(keep.shape[1:], f32)
    scores = []
    for part in (0, 1):
        for d in range(dates):
            inc, base = (
                jnp.where(first == (part == 0), keep[at], other[at]) for at in (d, dates + d)
            )
            run = run + inc
            scores.append(base - run)
    peak = functools.reduce(jnp.maximum, scores)
    lev = peak + jnp.log(sum(jnp.exp(s - peak) for s in scores))
    for i, s in enumerate(scores):
        score[i] = s
    level[...] = lev
    total[...] = run
    left = chip_of() % 2 == 0
    for i, m in enumerate(message_of(lev, run, left, rounds == 1)):
        message[i] = m


def merge_body(step, rounds, level, total, state, got, state2, message, *group):
    left = (chip_of() >> step) % 2 == 0
    lev, tot, other_lev, other_tot = level[...], total[...], got[0], got[1]
    if state is None:
        zero = jnp.zeros_like(lev)
        before, after, sum_before, sum_after = zero + NEG, zero + NEG, zero, zero
    else:
        before, after, sum_before, sum_after = (state[i] for i in range(4))
    state2[0] = jnp.where(left, before, log_add(before, other_lev + other_tot + sum_before))
    state2[1] = jnp.where(left, log_add(after, other_lev - sum_after), after)
    state2[2] = jnp.where(left, sum_before, sum_before + other_tot)
    state2[3] = jnp.where(left, sum_after + other_tot, sum_after)
    first_lev, first_tot = jnp.where(left, lev, other_lev), jnp.where(left, tot, other_tot)
    second_lev = jnp.where(left, other_lev, lev)
    lev2 = log_add(first_lev, second_lev - first_tot)
    tot2 = tot + other_tot
    for out, value in zip(group, (lev2, tot2)):
        out[...] = value
    next_left = (chip_of() >> (step + 1)) % 2 == 0
    for i, m in enumerate(message_of(lev2, tot2, next_left, step + 2 == rounds)):
        message[i] = m


def tail_body(rounds, score, level, total, state, got, out):
    lev, tot = level[...], total[...]
    zero = jnp.zeros_like(lev)
    if state is None:
        before, after, sum_before, sum_after = zero + NEG, zero + NEG, zero, zero
    else:
        before, after, sum_before, sum_after = (state[i] for i in range(4))
    if got is not None:
        left = (chip_of() >> (rounds - 1)) % 2 == 0
        other = got[0]
        before = jnp.where(left, before, log_add(before, other + sum_before))
        after = jnp.where(left, log_add(after, other - sum_after), after)
    later = after - tot
    norm = log_add(log_add(before, lev), later)
    run = jnp.exp(later - norm)
    half = score.shape[1]
    for i in reversed(range(score.shape[0])):
        run = run + jnp.exp(score[i] - norm)
        out[i * half : (i + 1) * half, :] = run.astype(bf16).astype(f32)
    smoothed = jnp.where(chip_of() == 0, TEMP * norm, 0.0)
    at = score.shape[0] * half
    out[at : at + STAT_ROWS, :] = jnp.zeros((STAT_ROWS, smoothed.shape[1]), f32)
    out[at : at + 1, :] = jnp.sum(smoothed, axis=0, keepdims=True)
    out[at + 1 : at + 2, :] = jnp.sum(smoothed * smoothed, axis=0, keepdims=True)


def halves_body(chips, features, send):
    width = features.shape[2] // (2 * chips)
    for z in range(chips):
        at = pl.multiple_of((2 * z + 1 - core_of()) * width, width)
        send[:, :, z * width : (z + 1) * width] = features[:, :, pl.ds(at, width)].astype(f32)


def columns_body(chips, features, got, columns):
    dates, paths, whole = features.shape
    width = whole // (2 * chips)
    mine, theirs = core_of() * dates, (1 - core_of()) * dates
    for z in range(chips):
        at = pl.multiple_of((2 * z + core_of()) * width, width)
        rows = slice(z * width, (z + 1) * width)
        for d in range(dates):
            own = features[d, :, pl.ds(at, width)].T
            columns[rows, pl.ds(pl.multiple_of((mine + d) * paths, paths), paths)] = own
            other = got[d, :, rows].astype(bf16).T
            columns[rows, pl.ds(pl.multiple_of((theirs + d) * paths, paths), paths)] = other


def gather_body(own, got, tail, stats):
    dates, paths, _ = tail.shape
    half = paths // 2
    for source, at in ((own, core_of()), (got, 1 - core_of())):
        rows = pl.ds(pl.multiple_of(at * half, half), half)
        for d in range(dates):
            tail[d, rows] = source[d * half : (d + 1) * half, :].astype(bf16)
    stats[...] = own[dates * half :, :] + got[dates * half :, :]


def product_body(scale, first_chip, columns, *refs):
    if first_chip == 0:
        own, got, keep, message, tail, stats, product = refs
        gather_body(own, got, tail, stats)
    else:
        tail, stats, keep, message, product = refs
    dates, paths, contracts = tail.shape
    right = tail[...].reshape(dates * paths, contracts)
    chips, count, rows, _ = product.shape
    width = count * rows
    for z in range(chips):
        at = (first_chip + z) * width
        block = jnp.dot(columns[at : at + width, :], right, preferred_element_type=f32)
        product[z] = (scale * block).reshape(count, rows, contracts)
    halve(0, product, stats[...], keep, message)


def path_bits(count):
    bits = list(range(count.bit_length() - 1))
    return bits, bits[len(bits) // 2 :] + bits[: len(bits) // 2]


def halve(step, product, stats, keep, message):
    chips, n, rows, _ = product.shape
    first, second = path_bits(lax.axis_size("path"))
    bit, place = (
        jnp.where(core_of() == 0, a, b)
        for a, b in (
            (first[step], second[step]),
            tuple(sum(x < order[step] for x in order[step + 1 :]) for order in (first, second)),
        )
    )
    mine = (lax.axis_index("path") >> bit) & 1
    for out, value in ((keep, mine), (message, 1 - mine)):
        for z in range(chips):
            for i in range(n // 2):
                low = i & ((1 << place) - 1)
                at = ((i - low) << 1) + (value << place) + low
                start = (z * (n // 2) + i) * rows
                out[start : start + rows, :] = product[z, at]
        out[chips * (n // 2) * rows :, :] = stats


def path_pairs(chips, count, step):
    first, second = path_bits(count)
    return [
        ((2 * z + core) * count + p, (2 * z + core) * count + (p ^ (1 << order[step])))
        for z in range(chips)
        for core, order in enumerate((first, second))
        for p in range(count)
    ]


def path_sum_body(step, mine, got, keep, message, product):
    chips, n, rows, contracts = product.shape
    size = chips * n * rows
    product[...] = (mine[:size, :] + got[:size, :]).reshape(product.shape)
    halve(step, product, mine[size:, :] + got[size:, :], keep, message)


def partner(me, j, count):
    if count & (count - 1) == 0:
        return me ^ j
    return lax.rem(me + j, count)


def pairs(count, j):
    if count & (count - 1) == 0:
        return [(i, i ^ j) for i in range(count)]
    return [(i, (i + j) % count) for i in range(count)]


def date_pairs(chips, j):
    return [(2 * a + core, 2 * b + core) for a, b in pairs(chips, j) for core in range(2)]


def chip_sum_body(chips, shares, *refs):
    given, (keep, *messages), (total,) = refs[: -chips - 1], refs[-chips - 1 : -1], refs[-1:]
    rows = (total.shape[0] - STAT_ROWS) // chips
    at = 0
    for part, share in enumerate(shares):
        mine, got = given[2 * part : 2 * part + 2]
        size = share * rows
        total[at : at + size, :] = mine[:size, :] + got[:size, :]
        at += size
    total[at:, :] = mine[size:, :] + got[size:, :]
    for j, out in enumerate((keep, *messages)):
        at = pl.multiple_of(partner(chip_of(), j, chips) * rows, rows)
        out[0:rows, :] = total[pl.ds(at, rows), :]
        out[rows:, :] = total[chips * rows :, :]


def date_sum_body(chips, paths_total, *refs):
    parts, (gradient, bound, spread) = refs[:chips], refs[chips:]
    total = functools.reduce(lambda a, b: a + b, (p[...] for p in parts))
    rows = gradient.shape[0]
    gradient[...] = total[:rows, :]
    mean = total[rows : rows + 1, :] * (1.0 / paths_total)
    bound[...] = mean
    spread[...] = total[rows + 1 : rows + 2, :] * (1.0 / paths_total) - mean * mean


def shards(features, payoff, coefficients, exercise):
    dates, paths, width = features.shape
    contracts = coefficients.shape[1]
    chips, count = lax.axis_size("date") // 2, lax.axis_size("path")
    rounds = chips.bit_length() - 1
    assert chips == 1 << rounds
    half, paths_total = paths // 2, paths * count
    rows = width // (2 * chips * count)
    cores = [(2 * z + c, 2 * z + 1 - c) for z in range(chips) for c in range(2)]
    plane = (half, contracts)

    keep, send, held = call(
        increments_body,
        [((2 * dates, *plane), f32), ((2 * dates, *plane), f32), (features.shape, bf16)],
        features,
        coefficients,
        payoff,
        exercise,
        scratch=[
            pltpu.VMEM((dates, paths, contracts), f32),
            pltpu.VMEM(coefficients.shape, bf16),
            pltpu.VMEM(payoff.shape, f32),
            pltpu.VMEM(exercise.shape, jnp.int32),
            pltpu.SemaphoreType.DMA((2 * PIECES + 2,)),
        ],
        flops=2 * dates * paths * width * contracts,
        place=pltpu.HBM,
    )
    other = lax.ppermute(send, "date", cores)
    sizes = [1 if step + 1 == rounds else 2 for step in range(rounds)] or [2]
    score, level, total, message = call(
        functools.partial(local_body, rounds),
        [((2 * dates, *plane), f32), (plane, f32), (plane, f32), ((sizes[0], *plane), f32)],
        keep,
        other,
    )
    (columns_send,) = call(
        functools.partial(halves_body, chips),
        [((dates, paths, width // 2), f32)],
        held,
        message,
        unread=1,
        flops=1 << 26,
    )
    own_level, own_total, state, got = level, total, None, None
    columns_got = lax.ppermute(columns_send, "date", cores)
    for step in range(rounds):
        got = lax.ppermute(message, "date", date_pairs(chips, 1 << step))
        if step + 1 == rounds:
            break
        body = functools.partial(merge_body, step, rounds)
        if state is None:
            body = lambda a, b, c, *o, body=body: body(a, b, None, c, *o)
        operands = [level, total, got] if state is None else [level, total, state, got]
        group = [(plane, f32)] * (0 if step + 2 == rounds else 2)
        state, message, *group = call(body, [((4, *plane), f32), ((sizes[step + 1], *plane), f32)] + group, *operands)
        level, total = group or (level, total)
    (columns,) = call(
        functools.partial(columns_body, chips),
        [((width // 2, 2 * dates * paths), bf16)],
        held,
        columns_got,
        message,
        unread=1,
        flops=1 << 27,
    )
    extra = [x for x in (state, got) if x is not None]

    def tail_kernel(score, level, total, *rest):
        rest = list(rest)
        given = rest.pop(0) if state is not None else None
        arrived = rest.pop(0) if got is not None else None
        tail_body(rounds, score, level, total, given, arrived, *rest)

    (tail,) = call(
        tail_kernel,
        [((2 * dates * half + STAT_ROWS, contracts), f32)],
        score,
        own_level,
        own_total,
        *extra,
    )
    tail_other = lax.ppermute(tail, "date", cores)
    steps = count.bit_length() - 1
    assert count == 1 << steps and steps > 0
    shares = (chips - chips // 4, chips // 4) if chips >= 4 else (chips,)

    def piece(n, chips):
        return ((chips * n * rows + STAT_ROWS, contracts), f32)

    sent = []
    for part, share in enumerate(shares):
        first = part == 0
        joined = [((2 * dates, paths, contracts), bf16), ((STAT_ROWS, contracts), f32)]
        keep, message, *made = call(
            functools.partial(product_body, -1.0 / paths_total, sum(shares[:part])),
            [piece(count // 2, share)] * 2 + (joined if first else []),
            columns,
            *([tail, tail_other] if first else gathered),
            scratch=[pltpu.VMEM((share, count, rows, contracts), f32)],
            flops=2 * dates * paths * width * contracts * share // chips,
        )
        gathered = made or gathered
        sent.append((keep, message))
    for step in range(steps):
        sent = [(keep, lax.ppermute(m, ("date", "path"), path_pairs(chips, count, step))) for keep, m in sent]
        if step + 1 == steps:
            break
        n = count >> (step + 1)
        sent = [
            call(
                functools.partial(path_sum_body, step + 1),
                [piece(n // 2, share)] * 2,
                *pair,
                scratch=[pltpu.VMEM((share, n, rows, contracts), f32)],
            )
            for share, pair in zip(shares, sent)
        ]
    pieces = call(
        functools.partial(chip_sum_body, chips, shares),
        [((rows + STAT_ROWS, contracts), f32)] * chips,
        *[x for pair in sent for x in pair],
        scratch=[pltpu.VMEM(*piece(1, chips))],
    )
    order = sorted(range(1, chips), key=lambda j: (-j.bit_length(), j))
    pieces = [pieces[0]] + [lax.ppermute(pieces[j], "date", date_pairs(chips, j)) for j in order]
    gradient, bound, spread = call(
        functools.partial(date_sum_body, chips, paths_total),
        [((rows, contracts), f32), ((1, contracts), f32), ((1, contracts), f32)],
        *pieces,
    )
    return gradient, bound.reshape(contracts), spread.reshape(contracts)


def solution(mesh):
    placed = (P("date", "path", None), P("date", "path", None), P(), P("date", None))
    return jax.shard_map(
        shards,
        mesh=mesh,
        in_specs=placed,
        out_specs=(P(("date", "path"), None), P(), P()),
        check_vma=False,
    )
```

```python
import functools

import jax
import jax.numpy as jnp
from jax import lax
from jax.experimental import pallas as pl
from jax.experimental.pallas import tpu as pltpu
from jax.sharding import PartitionSpec as P

INVERSE_TEMP = 4.0
TEMP = 0.25
NEG = -1e30
STAT_ROWS = 8
PIECES = 2
FIRST = 4
VMEM_LIMIT = 16 << 20
f32 = jnp.float32
bf16 = jnp.bfloat16


def core_of():
    return lax.axis_index("date") % 2


def chip_of():
    return lax.axis_index("date") // 2


def in_hbm(x):
    return pltpu.with_memory_space_constraint(x, pltpu.HBM)


def call(body, outs, *operands, scratch=(), flops=0, unread=0, place=()):
    whole = pl.BlockSpec(memory_space=pltpu.VMEM)
    anywhere = pl.BlockSpec(memory_space=pl.ANY)
    read = len(operands) - unread

    def kernel(*refs):
        body(*refs[:read], *refs[read + unread :])

    specs = [pl.BlockSpec(memory_space=p) for p in place]
    return pl.pallas_call(
        kernel,
        out_shape=[jax.ShapeDtypeStruct(*o) for o in outs],
        in_specs=specs + [whole] * (read - len(specs)) + [anywhere] * unread,
        out_specs=[whole] * len(outs),
        scratch_shapes=list(scratch),
        compiler_params=pltpu.CompilerParams(vmem_limit_bytes=VMEM_LIMIT),
        cost_estimate=pl.CostEstimate(flops=flops, bytes_accessed=0, transcendentals=0),
    )(*operands)


def log_add(a, b):
    return jnp.maximum(a, b) + jnp.log(1.0 + jnp.exp(-jnp.abs(a - b)))


def fill(out, inc, pay, may):
    dates = inc.shape[0]
    out[0:dates] = INVERSE_TEMP * inc
    for d in range(dates):
        out[dates + d] = jnp.where(may[d : d + 1, :] > 0, INVERSE_TEMP * pay[d], NEG)


def theirs_body(features, coefficients, payoff, exercise, send, held, weights, pay, may, sems, others):
    dates, paths, width = features.shape
    half, step = paths // 2, width // PIECES
    rows = pl.ds(pl.multiple_of((1 - core_of()) * half, half), half)
    parts = [slice(i * step, (i + 1) * step) for i in range(PIECES)]
    copies = [
        (
            pltpu.make_async_copy(features.at[:, rows, at], held.at[:, :, at], sems.at[2 * i]),
            pltpu.make_async_copy(coefficients.at[at, :], weights.at[at, :], sems.at[2 * i + 1]),
        )
        for i, at in enumerate(parts)
    ]
    small = (
        pltpu.make_async_copy(payoff.at[:, rows, :], pay, others.at[0]),
        pltpu.make_async_copy(exercise, may, others.at[1]),
    )
    for c in (*(c for pair in copies for c in pair), *small):
        c.start()
    inc = None
    for pair, at in zip(copies, parts):
        for c in pair:
            c.wait()
        left = held[:, :, at].reshape(dates * half, step)
        part = jnp.dot(left, weights[at, :], preferred_element_type=f32)
        inc = part if inc is None else inc + part
    for c in small:
        c.wait()
    fill(send, inc.reshape(dates, half, -1), pay, may)


def mine_body(features, payoff, exercise, weights, theirs, keep, held, pay, may, sems):
    dates, paths, width = features.shape
    half = paths // 2
    rows = pl.ds(pl.multiple_of(core_of() * half, half), half)
    copies = (
        pltpu.make_async_copy(features.at[:, rows, :], held.at[:, rows, :], sems.at[0]),
        pltpu.make_async_copy(payoff.at[:, rows, :], pay, sems.at[1]),
        pltpu.make_async_copy(exercise, may, sems.at[2]),
    )
    for c in copies:
        c.start()
    held[:, pl.ds(pl.multiple_of((1 - core_of()) * half, half), half), :] = theirs[...]
    for c in copies:
        c.wait()
    inc = jnp.dot(held[:, rows, :].reshape(dates * half, width), weights[...], preferred_element_type=f32)
    fill(keep, inc.reshape(dates, half, -1), pay, may)


def message_of(level, total, left, last):
    if last:
        return [jnp.where(left, level + total, level)]
    return [level, total]


def local_body(rounds, keep, other, score, level, total, message):
    dates = keep.shape[0] // 2
    first = core_of() == 0
    run = jnp.zeros(keep.shape[1:], f32)
    scores = []
    for part in (0, 1):
        for d in range(dates):
            inc, base = (
                jnp.where(first == (part == 0), keep[at], other[at]) for at in (d, dates + d)
            )
            run = run + inc
            scores.append(base - run)
    peak = functools.reduce(jnp.maximum, scores)
    lev = peak + jnp.log(sum(jnp.exp(s - peak) for s in scores))
    for i, s in enumerate(scores):
        score[i] = s
    level[...] = lev
    total[...] = run
    left = chip_of() % 2 == 0
    if rounds == 2:
        message[0] = jnp.where(left, lev + run, lev)
        return
    for i, m in enumerate(message_of(lev, run, left, rounds == 1)):
        message[i] = m


def pair_body(total, message, near, out):
    both = log_add(message[0], near[0])
    own = total[...]
    out[0] = both + jnp.where(chip_of() == 1, own, jnp.where(chip_of() == 2, -own, 0.0))


def merge_body(step, rounds, level, total, state, got, state2, message, *group):
    left = (chip_of() >> step) % 2 == 0
    lev, tot, other_lev, other_tot = level[...], total[...], got[0], got[1]
    if state is None:
        zero = jnp.zeros_like(lev)
        before, after, sum_before, sum_after = zero + NEG, zero + NEG, zero, zero
    else:
        before, after, sum_before, sum_after = (state[i] for i in range(4))
    state2[0] = jnp.where(left, before, log_add(before, other_lev + other_tot + sum_before))
    state2[1] = jnp.where(left, log_add(after, other_lev - sum_after), after)
    state2[2] = jnp.where(left, sum_before, sum_before + other_tot)
    state2[3] = jnp.where(left, sum_after + other_tot, sum_after)
    first_lev, first_tot = jnp.where(left, lev, other_lev), jnp.where(left, tot, other_tot)
    second_lev = jnp.where(left, other_lev, lev)
    lev2 = log_add(first_lev, second_lev - first_tot)
    tot2 = tot + other_tot
    for out, value in zip(group, (lev2, tot2)):
        out[...] = value
    next_left = (chip_of() >> (step + 1)) % 2 == 0
    for i, m in enumerate(message_of(lev2, tot2, next_left, step + 2 == rounds)):
        message[i] = m


def joined(rounds, state, got, zero):
    if state is None:
        before, after, sum_before, sum_after = zero + NEG, zero + NEG, zero, zero
    else:
        before, after, sum_before, sum_after = (state[i] for i in range(4))
    if got is not None:
        left = (chip_of() >> (rounds - 1)) % 2 == 0
        other = got[0]
        before = jnp.where(left, before, log_add(before, other + sum_before))
        after = jnp.where(left, log_add(after, other - sum_after), after)
    return before, after, sum_before


def joined_four(near, far, beside, across):
    first, left = chip_of() % 2 == 0, chip_of() < 2
    shift = jnp.where(first == left, beside[...], across[...])
    near, far = near[0], far[0] + jnp.where(left, -shift, shift)
    both, none = log_add(near, far), jnp.zeros_like(near) + NEG
    before = jnp.where(left, jnp.where(first, none, near), jnp.where(first, far, both))
    after = jnp.where(left, jnp.where(first, both, far), jnp.where(first, near, none))
    return before, after, jnp.where(first, 0.0, beside[...])


def tail_body(join, score, level, total, *refs):
    *given, out = refs
    lev, tot = level[...], total[...]
    before, after, sum_before = join(*given, jnp.zeros_like(lev))
    later = after - tot
    norm = log_add(log_add(before, lev), later)
    run = jnp.exp(later - norm)
    half = score.shape[1]
    for i in reversed(range(score.shape[0])):
        run = run + jnp.exp(score[i] - norm)
        out[i * half : (i + 1) * half, :] = run.astype(bf16).astype(f32)
    smoothed = TEMP * (norm - sum_before)
    at = score.shape[0] * half
    out[at : at + STAT_ROWS, :] = jnp.zeros((STAT_ROWS, smoothed.shape[1]), f32)
    out[at : at + 1, :] = jnp.sum(smoothed, axis=0, keepdims=True)
    out[at + 1 : at + 2, :] = jnp.sum(smoothed * smoothed, axis=0, keepdims=True)


def halves_body(chips, features, send):
    width = features.shape[2] // (2 * chips)
    for z in range(chips):
        at = pl.multiple_of((2 * z + 1 - core_of()) * width, width)
        send[:, :, z * width : (z + 1) * width] = features[:, :, pl.ds(at, width)].astype(f32)


def columns_body(chips, features, got, columns):
    dates, paths, whole = features.shape
    half, width = paths // 2, whole // (2 * chips)
    size = dates * half
    for z in range(chips):
        at = pl.multiple_of((2 * z + core_of()) * width, width)
        rows = slice(z * width, (z + 1) * width)
        for h in range(2):
            span = slice(h * half, (h + 1) * half)
            own = features[:, span, pl.ds(at, width)].reshape(size, width).T
            columns[rows, pl.ds(pl.multiple_of((2 * h + core_of()) * size, size), size)] = own
            other = got[:, span, rows].astype(bf16).reshape(size, width).T
            columns[rows, pl.ds(pl.multiple_of((2 * h + 1 - core_of()) * size, size), size)] = other


def side(columns, rows, half):
    size = columns.shape[1] // 2
    return columns[rows, pl.ds(pl.multiple_of(half * size, size), size)]


def first_body(scale, columns, own, out):
    size = columns.shape[1] // 2
    right = own[:size, :].astype(bf16)
    step = columns.shape[0] // FIRST
    for i in range(FIRST):
        rows = slice(i * step, (i + 1) * step)
        out[rows, :] = scale * jnp.dot(side(columns, rows, core_of()), right, preferred_element_type=f32)


def product_body(scale, first_chip, columns, begun, own, got, keep, message, product):
    size = columns.shape[1] // 2
    right = got[:size, :].astype(bf16)
    chips, count, rows, contracts = product.shape
    width = count * rows
    for z in range(chips):
        at = slice((first_chip + z) * width, (first_chip + z + 1) * width)
        block = scale * jnp.dot(side(columns, at, 1 - core_of()), right, preferred_element_type=f32)
        product[z] = (begun[at, :] + block).reshape(count, rows, contracts)
    halve(0, product, own[size:, :] + got[size:, :], keep, message)


def path_bits(count):
    bits = list(range(count.bit_length() - 1))
    return bits, bits[len(bits) // 2 :] + bits[: len(bits) // 2]


def halve(step, product, stats, keep, message):
    chips, n, rows, _ = product.shape
    first, second = path_bits(lax.axis_size("path"))
    bit, place = (
        jnp.where(core_of() == 0, a, b)
        for a, b in (
            (first[step], second[step]),
            tuple(sum(x < order[step] for x in order[step + 1 :]) for order in (first, second)),
        )
    )
    mine = (lax.axis_index("path") >> bit) & 1
    for out, value in ((keep, mine), (message, 1 - mine)):
        for z in range(chips):
            for i in range(n // 2):
                low = i & ((1 << place) - 1)
                at = ((i - low) << 1) + (value << place) + low
                start = (z * (n // 2) + i) * rows
                out[start : start + rows, :] = product[z, at]
        out[chips * (n // 2) * rows :, :] = stats


def path_pairs(chips, count, step):
    first, second = path_bits(count)
    return [
        ((2 * z + core) * count + p, (2 * z + core) * count + (p ^ (1 << order[step])))
        for z in range(chips)
        for core, order in enumerate((first, second))
        for p in range(count)
    ]


def path_sum_body(step, mine, got, keep, message, product):
    chips, n, rows, contracts = product.shape
    size = chips * n * rows
    product[...] = (mine[:size, :] + got[:size, :]).reshape(product.shape)
    halve(step, product, mine[size:, :] + got[size:, :], keep, message)


def partner(me, j, count):
    if count & (count - 1) == 0:
        return me ^ j
    return lax.rem(me + j, count)


def pairs(count, j):
    if count & (count - 1) == 0:
        return [(i, i ^ j) for i in range(count)]
    return [(i, (i + j) % count) for i in range(count)]


def date_pairs(chips, j):
    return [(2 * a + core, 2 * b + core) for a, b in pairs(chips, j) for core in range(2)]


def chip_sum_body(chips, shares, *refs):
    given, (keep, *messages), (total,) = refs[: -chips - 1], refs[-chips - 1 : -1], refs[-1:]
    rows = (total.shape[0] - STAT_ROWS) // chips
    at = 0
    for part, share in enumerate(shares):
        mine, got = given[2 * part : 2 * part + 2]
        size = share * rows
        total[at : at + size, :] = mine[:size, :] + got[:size, :]
        at += size
    total[at:, :] = mine[size:, :] + got[size:, :]
    for j, out in enumerate((keep, *messages)):
        at = pl.multiple_of(partner(chip_of(), j, chips) * rows, rows)
        out[0:rows, :] = total[pl.ds(at, rows), :]
        if out.shape[0] > rows:
            out[rows:, :] = total[chips * rows :, :]


def date_sum_body(chips, paths_total, *refs):
    parts, (gradient, bound, spread) = refs[:chips], refs[chips:]
    rows = gradient.shape[0]
    gradient[...] = functools.reduce(lambda a, b: a + b, (p[:rows, :] for p in parts))
    first = chip_of() < max(chips // 2, 1)
    across = parts[([0] + chip_order(chips)).index(chips // 2)]
    stats = jnp.where(first, parts[0][rows:, :], across[rows:, :])
    mean = stats[0:1, :] * (1.0 / paths_total)
    bound[...] = mean
    spread[...] = stats[1:2, :] * (1.0 / paths_total) - mean * mean


def chip_order(chips):
    return sorted(range(1, chips), key=lambda j: (-j.bit_length(), j))


def shards(features, payoff, coefficients, exercise):
    dates, paths, width = features.shape
    contracts = coefficients.shape[1]
    chips, count = lax.axis_size("date") // 2, lax.axis_size("path")
    rounds = chips.bit_length() - 1
    assert chips == 1 << rounds
    half, paths_total = paths // 2, paths * count
    rows = width // (2 * chips * count)
    cores = [(2 * z + c, 2 * z + 1 - c) for z in range(chips) for c in range(2)]
    plane = (half, contracts)

    halves = (dates, half, width)
    send, theirs, weights = call(
        theirs_body,
        [((2 * dates, *plane), f32), (halves, bf16), (coefficients.shape, bf16)],
        *(in_hbm(x) for x in (features, coefficients, payoff, exercise)),
        scratch=[
            pltpu.VMEM((dates, half, contracts), f32),
            pltpu.VMEM(exercise.shape, jnp.int32),
            pltpu.SemaphoreType.DMA((2 * PIECES,)),
            pltpu.SemaphoreType.DMA((2,)),
        ],
        place=[pltpu.HBM] * 4,
    )
    other = lax.ppermute(send, "date", cores)
    keep, held = call(
        mine_body,
        [((2 * dates, *plane), f32), (features.shape, bf16)],
        *(in_hbm(x) for x in (features, payoff, exercise)),
        weights,
        theirs,
        scratch=[
            pltpu.VMEM((dates, half, contracts), f32),
            pltpu.VMEM(exercise.shape, jnp.int32),
            pltpu.SemaphoreType.DMA((3,)),
        ],
        place=[pltpu.HBM] * 3,
    )
    sizes = [1 if step + 1 == rounds or rounds == 2 else 2 for step in range(rounds)] or [2]
    score, level, total, message = call(
        functools.partial(local_body, rounds),
        [((2 * dates, *plane), f32), (plane, f32), (plane, f32), ((sizes[0], *plane), f32)],
        keep,
        other,
    )
    (columns_send,) = call(
        functools.partial(halves_body, chips),
        [((dates, paths, width // 2), f32)],
        held,
        message,
        unread=1,
    )
    columns_got = lax.ppermute(columns_send, "date", cores)
    own_level, own_total, state, got = level, total, None, None
    if rounds == 2:
        near = lax.ppermute(message, "date", date_pairs(chips, 1))
        beside = lax.ppermute(total, "date", date_pairs(chips, 1))
        across = lax.ppermute(total, "date", [(2 * a + c, 6 - 2 * a + c) for a in (1, 2) for c in range(2)])
        (message,) = call(pair_body, [((1, *plane), f32)], total, message, near)
        far = lax.ppermute(message, "date", date_pairs(chips, 2))
        given, turn = [near, far, beside, across], [beside, across]
        join = lambda *refs: joined_four(*refs[:4])
    else:
        for step in range(rounds):
            got = lax.ppermute(message, "date", date_pairs(chips, 1 << step))
            if step + 1 == rounds:
                break
            body = functools.partial(merge_body, step, rounds)
            if state is None:
                body = lambda a, b, c, *o, body=body: body(a, b, None, c, *o)
            operands = [level, total, got] if state is None else [level, total, state, got]
            group = [(plane, f32)] * (0 if step + 2 == rounds else 2)
            state, message, *group = call(
                body, [((4, *plane), f32), ((sizes[step + 1], *plane), f32)] + group, *operands
            )
            level, total = group or (level, total)
        given, turn = [x for x in (state, got) if x is not None], [message]

        def join(*refs, joined=joined):
            *refs, zero = refs
            held = refs[0] if state is not None else None
            return joined(rounds, held, refs[-1] if got is not None else None, zero)

    (columns,) = call(
        functools.partial(columns_body, chips),
        [((width // 2, 2 * dates * paths), bf16)],
        held,
        columns_got,
        *turn,
        unread=len(turn),
        flops=1 << 27,
    )
    (tail,) = call(
        functools.partial(tail_body, join),
        [((2 * dates * half + STAT_ROWS, contracts), f32)],
        score,
        own_level,
        own_total,
        *given,
        columns,
        unread=1,
    )
    tail_other = lax.ppermute(tail, "date", cores)
    steps = count.bit_length() - 1
    assert count == 1 << steps and steps > 0
    shares = (chips - chips // 4, chips // 4) if chips >= 4 else (chips,)

    def piece(n, chips):
        return ((chips * n * rows + STAT_ROWS, contracts), f32)

    (begun,) = call(
        functools.partial(first_body, -1.0 / paths_total),
        [((width // 2, contracts), f32)],
        columns,
        tail,
        flops=dates * paths * width * contracts,
    )
    sent = [
        call(
            functools.partial(product_body, -1.0 / paths_total, sum(shares[:part])),
            [piece(count // 2, share)] * 2,
            columns,
            begun,
            tail,
            tail_other,
            scratch=[pltpu.VMEM((share, count, rows, contracts), f32)],
            flops=dates * paths * width * contracts * share // chips,
        )
        for part, share in enumerate(shares)
    ]
    for step in range(steps):
        sent = [(keep, lax.ppermute(m, ("date", "path"), path_pairs(chips, count, step))) for keep, m in sent]
        if step + 1 == steps:
            break
        n = count >> (step + 1)
        sent = [
            call(
                functools.partial(path_sum_body, step + 1),
                [piece(n // 2, share)] * 2,
                *pair,
                scratch=[pltpu.VMEM((share, n, rows, contracts), f32)],
            )
            for share, pair in zip(shares, sent)
        ]
    pieces = call(
        functools.partial(chip_sum_body, chips, shares),
        [((rows + (STAT_ROWS if j in (0, chips // 2) else 0), contracts), f32) for j in range(chips)],
        *[x for pair in sent for x in pair],
        scratch=[pltpu.VMEM(*piece(1, chips))],
    )
    over = {j: lax.ppermute(pieces[j], "date", date_pairs(chips, j)) for j in chip_order(chips)}
    pieces = [pieces[0]] + list(over.values())
    gradient, bound, spread = call(
        functools.partial(date_sum_body, chips, paths_total),
        [((rows, contracts), f32), ((1, contracts), f32), ((1, contracts), f32)],
        *pieces,
    )
    return gradient, bound.reshape(contracts), spread.reshape(contracts)


def solution(mesh):
    placed = (P("date", "path", None), P("date", "path", None), P(), P("date", None))
    return jax.shard_map(
        shards,
        mesh=mesh,
        in_specs=placed,
        out_specs=(P(("date", "path"), None), P(), P()),
        check_vma=False,
    )
```

```python
import functools

import jax
import jax.numpy as jnp
from jax import lax
from jax.experimental import pallas as pl
from jax.experimental.pallas import tpu as pltpu
from jax.sharding import PartitionSpec as P

INVERSE_TEMP = 4.0
TEMP = 0.25
NEG = -1e30
STAT_ROWS = 8
PIECES = 2
FIRST = 4
FIRST_ROWS = 5
VMEM_LIMIT = 16 << 20
f32 = jnp.float32
bf16 = jnp.bfloat16


def core_of():
    return lax.axis_index("date") % 2


def chip_of():
    return lax.axis_index("date") // 2


def in_hbm(x):
    return pltpu.with_memory_space_constraint(x, pltpu.HBM)


def call(body, outs, *operands, scratch=(), flops=0, unread=0, place=()):
    whole = pl.BlockSpec(memory_space=pltpu.VMEM)
    anywhere = pl.BlockSpec(memory_space=pl.ANY)
    read = len(operands) - unread

    def kernel(*refs):
        body(*refs[:read], *refs[read + unread :])

    specs = [pl.BlockSpec(memory_space=p) for p in place]
    return pl.pallas_call(
        kernel,
        out_shape=[jax.ShapeDtypeStruct(*o) for o in outs],
        in_specs=specs + [whole] * (read - len(specs)) + [anywhere] * unread,
        out_specs=[whole] * len(outs),
        scratch_shapes=list(scratch),
        compiler_params=pltpu.CompilerParams(vmem_limit_bytes=VMEM_LIMIT),
        cost_estimate=pl.CostEstimate(flops=flops, bytes_accessed=0, transcendentals=0),
    )(*operands)


def log_add(a, b):
    return jnp.maximum(a, b) + jnp.log(1.0 + jnp.exp(-jnp.abs(a - b)))


def fill(out, inc, pay, may):
    dates = inc.shape[0]
    out[0:dates] = INVERSE_TEMP * inc
    for d in range(dates):
        out[dates + d] = jnp.where(may[d : d + 1, :] > 0, INVERSE_TEMP * pay[d], NEG)


def theirs_body(features, coefficients, payoff, exercise, send, held, weights, pay, may, sems, others):
    dates, paths, width = features.shape
    half, step = paths // 2, width // PIECES
    rows = pl.ds(pl.multiple_of((1 - core_of()) * half, half), half)
    parts = [slice(i * step, (i + 1) * step) for i in range(PIECES)]
    copies = [
        (
            pltpu.make_async_copy(features.at[:, rows, at], held.at[:, :, at], sems.at[2 * i]),
            pltpu.make_async_copy(coefficients.at[at, :], weights.at[at, :], sems.at[2 * i + 1]),
        )
        for i, at in enumerate(parts)
    ]
    small = (
        pltpu.make_async_copy(payoff.at[:, rows, :], pay, others.at[0]),
        pltpu.make_async_copy(exercise, may, others.at[1]),
    )
    for c in (*(c for pair in copies for c in pair), *small):
        c.start()
    inc = None
    for pair, at in zip(copies, parts):
        for c in pair:
            c.wait()
        left = held[:, :, at].reshape(dates * half, step)
        part = jnp.dot(left, weights[at, :], preferred_element_type=f32)
        inc = part if inc is None else inc + part
    for c in small:
        c.wait()
    fill(send, inc.reshape(dates, half, -1), pay, may)


def mine_body(features, payoff, exercise, weights, theirs, keep, held, pay, may, sems):
    dates, paths, width = features.shape
    half = paths // 2
    rows = pl.ds(pl.multiple_of(core_of() * half, half), half)
    copies = (
        pltpu.make_async_copy(features.at[:, rows, :], held.at[:, rows, :], sems.at[0]),
        pltpu.make_async_copy(payoff.at[:, rows, :], pay, sems.at[1]),
        pltpu.make_async_copy(exercise, may, sems.at[2]),
    )
    for c in copies:
        c.start()
    held[:, pl.ds(pl.multiple_of((1 - core_of()) * half, half), half), :] = theirs[...]
    for c in copies:
        c.wait()
    inc = jnp.dot(held[:, rows, :].reshape(dates * half, width), weights[...], preferred_element_type=f32)
    fill(keep, inc.reshape(dates, half, -1), pay, may)


def message_of(level, total, left, last):
    if last:
        return [jnp.where(left, level + total, level)]
    return [level, total]


def local_body(rounds, keep, other, score, level, total, message):
    dates = keep.shape[0] // 2
    first = core_of() == 0
    run = jnp.zeros(keep.shape[1:], f32)
    scores = []
    for part in (0, 1):
        for d in range(dates):
            inc, base = (
                jnp.where(first == (part == 0), keep[at], other[at]) for at in (d, dates + d)
            )
            run = run + inc
            scores.append(base - run)
    peak = functools.reduce(jnp.maximum, scores)
    lev = peak + jnp.log(sum(jnp.exp(s - peak) for s in scores))
    for i, s in enumerate(scores):
        score[i] = s
    level[...] = lev
    total[...] = run
    left = chip_of() % 2 == 0
    if rounds == 2:
        message[0] = jnp.where(left, lev + run, lev)
        return
    for i, m in enumerate(message_of(lev, run, left, rounds == 1)):
        message[i] = m


def pair_body(total, message, near, out):
    both = log_add(message[0], near[0])
    own = total[...]
    out[0] = both + jnp.where(chip_of() == 1, own, jnp.where(chip_of() == 2, -own, 0.0))


def merge_body(step, rounds, level, total, state, got, state2, message, *group):
    left = (chip_of() >> step) % 2 == 0
    lev, tot, other_lev, other_tot = level[...], total[...], got[0], got[1]
    if state is None:
        zero = jnp.zeros_like(lev)
        before, after, sum_before, sum_after = zero + NEG, zero + NEG, zero, zero
    else:
        before, after, sum_before, sum_after = (state[i] for i in range(4))
    state2[0] = jnp.where(left, before, log_add(before, other_lev + other_tot + sum_before))
    state2[1] = jnp.where(left, log_add(after, other_lev - sum_after), after)
    state2[2] = jnp.where(left, sum_before, sum_before + other_tot)
    state2[3] = jnp.where(left, sum_after + other_tot, sum_after)
    first_lev, first_tot = jnp.where(left, lev, other_lev), jnp.where(left, tot, other_tot)
    second_lev = jnp.where(left, other_lev, lev)
    lev2 = log_add(first_lev, second_lev - first_tot)
    tot2 = tot + other_tot
    for out, value in zip(group, (lev2, tot2)):
        out[...] = value
    next_left = (chip_of() >> (step + 1)) % 2 == 0
    for i, m in enumerate(message_of(lev2, tot2, next_left, step + 2 == rounds)):
        message[i] = m


def joined(rounds, state, got, zero):
    if state is None:
        before, after, sum_before, sum_after = zero + NEG, zero + NEG, zero, zero
    else:
        before, after, sum_before, sum_after = (state[i] for i in range(4))
    if got is not None:
        left = (chip_of() >> (rounds - 1)) % 2 == 0
        other = got[0]
        before = jnp.where(left, before, log_add(before, other + sum_before))
        after = jnp.where(left, log_add(after, other - sum_after), after)
    return before, after, sum_before


def joined_four(near, far, beside, across):
    first, left = chip_of() % 2 == 0, chip_of() < 2
    shift = jnp.where(first == left, beside[...], across[...])
    near, far = near[0], far[0] + jnp.where(left, -shift, shift)
    both, none = log_add(near, far), jnp.zeros_like(near) + NEG
    before = jnp.where(left, jnp.where(first, none, near), jnp.where(first, far, both))
    after = jnp.where(left, jnp.where(first, both, far), jnp.where(first, near, none))
    return before, after, jnp.where(first, 0.0, beside[...])


def tail_body(join, score, level, total, *refs):
    *given, out = refs
    lev, tot = level[...], total[...]
    before, after, sum_before = join(*given, jnp.zeros_like(lev))
    later = after - tot
    norm = log_add(log_add(before, lev), later)
    run = jnp.exp(later - norm)
    half = score.shape[1]
    for i in reversed(range(score.shape[0])):
        run = run + jnp.exp(score[i] - norm)
        out[i * half : (i + 1) * half, :] = run.astype(bf16).astype(f32)
    smoothed = TEMP * (norm - sum_before)
    at = score.shape[0] * half
    out[at : at + STAT_ROWS, :] = jnp.zeros((STAT_ROWS, smoothed.shape[1]), f32)
    out[at : at + 1, :] = jnp.sum(smoothed, axis=0, keepdims=True)
    out[at + 1 : at + 2, :] = jnp.sum(smoothed * smoothed, axis=0, keepdims=True)


def halves_body(chips, features, send):
    width = features.shape[2] // (2 * chips)
    for z in range(chips):
        at = pl.multiple_of((2 * z + 1 - core_of()) * width, width)
        send[:, :, z * width : (z + 1) * width] = features[:, :, pl.ds(at, width)].astype(f32)


def columns_body(chips, features, got, columns):
    dates, paths, whole = features.shape
    half, width = paths // 2, whole // (2 * chips)
    size = dates * half
    for z in range(chips):
        at = pl.multiple_of((2 * z + core_of()) * width, width)
        rows = slice(z * width, (z + 1) * width)
        for h in range(2):
            span = slice(h * half, (h + 1) * half)
            own = features[:, span, pl.ds(at, width)].reshape(size, width).T
            columns[rows, pl.ds(pl.multiple_of((2 * h + core_of()) * size, size), size)] = own
            other = got[:, span, rows].astype(bf16).reshape(size, width).T
            columns[rows, pl.ds(pl.multiple_of((2 * h + 1 - core_of()) * size, size), size)] = other


def side(columns, rows, half):
    size = columns.shape[1] // 2
    return columns[rows, pl.ds(pl.multiple_of(half * size, size), size)]


def first_body(scale, columns, own, out):
    size = columns.shape[1] // 2
    right = own[:size, :].astype(bf16)
    step = columns.shape[0] // FIRST
    for i in range(FIRST):
        rows = slice(i * step, (i + 1) * step)
        out[rows, :] = scale * jnp.dot(side(columns, rows, core_of()), right, preferred_element_type=f32)


def product_body(scale, cuts, columns, begun, own, got, *refs):
    *outs, product = refs
    size = columns.shape[1] // 2
    right = got[:size, :].astype(bf16)
    chips, count, rows, contracts = product.shape
    width = count * rows
    for z in range(chips):
        at = slice(z * width, (z + 1) * width)
        block = scale * jnp.dot(side(columns, at, 1 - core_of()), right, preferred_element_type=f32)
        product[z] = (begun[at, :] + block).reshape(count, rows, contracts)
    stats = own[size:, :] + got[size:, :]
    for part, cut in enumerate(cuts):
        last = part + 1 == len(cuts)
        halve(0, product, cut, stats if last else None, *outs[2 * part : 2 * part + 2])


def path_bits(count):
    bits = list(range(count.bit_length() - 1))
    return bits, bits[len(bits) // 2 :] + bits[: len(bits) // 2]


def halve(step, product, cut, stats, keep, message):
    chips, n, _, _ = product.shape
    rows = cut.stop - cut.start
    first, second = path_bits(lax.axis_size("path"))
    bit, place = (
        jnp.where(core_of() == 0, a, b)
        for a, b in (
            (first[step], second[step]),
            tuple(sum(x < order[step] for x in order[step + 1 :]) for order in (first, second)),
        )
    )
    mine = (lax.axis_index("path") >> bit) & 1
    for out, value in ((keep, mine), (message, 1 - mine)):
        for z in range(chips):
            for i in range(n // 2):
                low = i & ((1 << place) - 1)
                at = ((i - low) << 1) + (value << place) + low
                start = (z * (n // 2) + i) * rows
                out[start : start + rows, :] = product[z, at, cut, :]
        if stats is not None:
            out[chips * (n // 2) * rows :, :] = stats


def path_pairs(chips, count, step):
    first, second = path_bits(count)
    return [
        ((2 * z + core) * count + p, (2 * z + core) * count + (p ^ (1 << order[step])))
        for z in range(chips)
        for core, order in enumerate((first, second))
        for p in range(count)
    ]


def path_sum_body(step, mine, got, keep, message, product):
    chips, n, rows, _ = product.shape
    size = chips * n * rows
    product[...] = (mine[:size, :] + got[:size, :]).reshape(product.shape)
    stats = mine[size:, :] + got[size:, :] if mine.shape[0] > size else None
    halve(step, product, slice(0, rows), stats, keep, message)


def partner(me, j, count):
    if count & (count - 1) == 0:
        return me ^ j
    return lax.rem(me + j, count)


def pairs(count, j):
    if count & (count - 1) == 0:
        return [(i, i ^ j) for i in range(count)]
    return [(i, (i + j) % count) for i in range(count)]


def date_pairs(chips, j):
    return [(2 * a + core, 2 * b + core) for a, b in pairs(chips, j) for core in range(2)]


def inner_pairs():
    inner = [(2 * a + c, 6 - 2 * a + c) for a in (1, 2) for c in range(2)]
    return inner + [(2 * a + c, 2 * a + 1 - c) for a in (0, 3) for c in range(2)]


def chip_sum_body(chips, cuts, *refs):
    given, (keep, *messages), (total,) = refs[: -chips - 1], refs[-chips - 1 : -1], refs[-1:]
    rows = (total.shape[0] - STAT_ROWS) // chips
    for part, cut in enumerate(cuts):
        mine, got = given[2 * part : 2 * part + 2]
        share = cut.stop - cut.start
        for z in range(chips):
            at = slice(z * share, (z + 1) * share)
            total[z * rows + cut.start : z * rows + cut.stop, :] = mine[at, :] + got[at, :]
    total[chips * rows :, :] = mine[chips * share :, :] + got[chips * share :, :]
    for j, out in enumerate((keep, *messages)):
        at = pl.multiple_of(partner(chip_of(), j, chips) * rows, rows)
        out[0:rows, :] = total[pl.ds(at, rows), :]
        if out.shape[0] > rows:
            out[rows:, :] = total[chips * rows :, :]


def date_sum_body(chips, paths_total, *refs):
    parts, (gradient, bound, spread) = refs[:chips], refs[chips:]
    rows = gradient.shape[0]
    gradient[...] = functools.reduce(lambda a, b: a + b, (p[:rows, :] for p in parts))
    first = chip_of() < max(chips // 2, 1)
    across = parts[([0] + chip_order(chips)).index(chips // 2)]
    stats = jnp.where(first, parts[0][rows:, :], across[rows:, :])
    mean = stats[0:1, :] * (1.0 / paths_total)
    bound[...] = mean
    spread[...] = stats[1:2, :] * (1.0 / paths_total) - mean * mean


def chip_order(chips):
    return sorted(range(1, chips), key=lambda j: (-j.bit_length(), j))


def shards(features, payoff, coefficients, exercise):
    dates, paths, width = features.shape
    contracts = coefficients.shape[1]
    chips, count = lax.axis_size("date") // 2, lax.axis_size("path")
    rounds = chips.bit_length() - 1
    assert chips == 1 << rounds
    half, paths_total = paths // 2, paths * count
    rows = width // (2 * chips * count)
    cores = [(2 * z + c, 2 * z + 1 - c) for z in range(chips) for c in range(2)]
    plane = (half, contracts)

    halves = (dates, half, width)
    send, theirs, weights = call(
        theirs_body,
        [((2 * dates, *plane), f32), (halves, bf16), (coefficients.shape, bf16)],
        *(in_hbm(x) for x in (features, coefficients, payoff, exercise)),
        scratch=[
            pltpu.VMEM((dates, half, contracts), f32),
            pltpu.VMEM(exercise.shape, jnp.int32),
            pltpu.SemaphoreType.DMA((2 * PIECES,)),
            pltpu.SemaphoreType.DMA((2,)),
        ],
        place=[pltpu.HBM] * 4,
    )
    other = lax.ppermute(send, "date", cores)
    keep, held = call(
        mine_body,
        [((2 * dates, *plane), f32), (features.shape, bf16)],
        *(in_hbm(x) for x in (features, payoff, exercise)),
        weights,
        theirs,
        scratch=[
            pltpu.VMEM((dates, half, contracts), f32),
            pltpu.VMEM(exercise.shape, jnp.int32),
            pltpu.SemaphoreType.DMA((3,)),
        ],
        place=[pltpu.HBM] * 3,
    )
    sizes = [1 if step + 1 == rounds or rounds == 2 else 2 for step in range(rounds)] or [2]
    score, level, total, message = call(
        functools.partial(local_body, rounds),
        [((2 * dates, *plane), f32), (plane, f32), (plane, f32), ((sizes[0], *plane), f32)],
        keep,
        other,
    )
    (columns_send,) = call(
        functools.partial(halves_body, chips),
        [((dates, paths, width // 2), f32)],
        held,
        message,
        unread=1,
    )
    columns_got = lax.ppermute(columns_send, "date", cores)
    own_level, own_total, state, got = level, total, None, None
    if rounds == 2:
        near = lax.ppermute(message, "date", date_pairs(chips, 1))
        beside = lax.ppermute(total, "date", date_pairs(chips, 1))
        across = lax.ppermute(total, "date", inner_pairs())
        (message,) = call(pair_body, [((1, *plane), f32)], total, message, near)
        far = lax.ppermute(message, "date", date_pairs(chips, 2))
        given, turn = [near, far, beside, across], [beside, across]
        join = lambda *refs: joined_four(*refs[:4])
    else:
        for step in range(rounds):
            got = lax.ppermute(message, "date", date_pairs(chips, 1 << step))
            if step + 1 == rounds:
                break
            body = functools.partial(merge_body, step, rounds)
            if state is None:
                body = lambda a, b, c, *o, body=body: body(a, b, None, c, *o)
            operands = [level, total, got] if state is None else [level, total, state, got]
            group = [(plane, f32)] * (0 if step + 2 == rounds else 2)
            state, message, *group = call(
                body, [((4, *plane), f32), ((sizes[step + 1], *plane), f32)] + group, *operands
            )
            level, total = group or (level, total)
        given, turn = [x for x in (state, got) if x is not None], [message]

        def join(*refs, joined=joined):
            *refs, zero = refs
            held = refs[0] if state is not None else None
            return joined(rounds, held, refs[-1] if got is not None else None, zero)

    (columns,) = call(
        functools.partial(columns_body, chips),
        [((width // 2, 2 * dates * paths), bf16)],
        held,
        columns_got,
        *turn,
        unread=len(turn),
        flops=1 << 27,
    )
    (tail,) = call(
        functools.partial(tail_body, join),
        [((2 * dates * half + STAT_ROWS, contracts), f32)],
        score,
        own_level,
        own_total,
        *given,
        columns,
        unread=1,
    )
    tail_other = lax.ppermute(tail, "date", cores)
    steps = count.bit_length() - 1
    assert count == 1 << steps and steps > 0
    first = rows * FIRST_ROWS // 8 // 8 * 8
    cuts = [slice(0, first), slice(first, rows)] if first else [slice(0, rows)]

    def piece(n, cut):
        stats = STAT_ROWS if cut is cuts[-1] else 0
        return ((chips * n * (cut.stop - cut.start) + stats, contracts), f32)

    (begun,) = call(
        functools.partial(first_body, -1.0 / paths_total),
        [((width // 2, contracts), f32)],
        columns,
        tail,
        flops=dates * paths * width * contracts,
    )
    outs = call(
        functools.partial(product_body, -1.0 / paths_total, cuts),
        [piece(count // 2, cut) for cut in cuts for _ in range(2)],
        columns,
        begun,
        tail,
        tail_other,
        scratch=[pltpu.VMEM((chips, count, rows, contracts), f32)],
        flops=dates * paths * width * contracts,
    )
    sent = [outs[2 * part : 2 * part + 2] for part in range(len(cuts))]
    for step in range(steps):
        sent = [(keep, lax.ppermute(m, ("date", "path"), path_pairs(chips, count, step))) for keep, m in sent]
        if step + 1 == steps:
            break
        n = count >> (step + 1)
        sent = [
            call(
                functools.partial(path_sum_body, step + 1),
                [piece(n // 2, cut)] * 2,
                *pair,
                scratch=[pltpu.VMEM((chips, n, cut.stop - cut.start, contracts), f32)],
            )
            for cut, pair in zip(cuts, sent)
        ]
    pieces = call(
        functools.partial(chip_sum_body, chips, cuts),
        [((rows + (STAT_ROWS if j in (0, chips // 2) else 0), contracts), f32) for j in range(chips)],
        *[x for pair in sent for x in pair],
        scratch=[pltpu.VMEM((chips * rows + STAT_ROWS, contracts), f32)],
    )
    over = {j: lax.ppermute(pieces[j], "date", date_pairs(chips, j)) for j in chip_order(chips)}
    pieces = [pieces[0]] + list(over.values())
    gradient, bound, spread = call(
        functools.partial(date_sum_body, chips, paths_total),
        [((rows, contracts), f32), ((1, contracts), f32), ((1, contracts), f32)],
        *pieces,
    )
    return gradient, bound.reshape(contracts), spread.reshape(contracts)


def solution(mesh):
    placed = (P("date", "path", None), P("date", "path", None), P(), P("date", None))
    return jax.shard_map(
        shards,
        mesh=mesh,
        in_specs=placed,
        out_specs=(P(("date", "path"), None), P(), P()),
        check_vma=False,
    )
```

```python
import functools

import jax
import jax.numpy as jnp
from jax import lax
from jax.experimental import pallas as pl
from jax.experimental.pallas import tpu as pltpu
from jax.sharding import PartitionSpec as P

INVERSE_TEMP = 4.0
TEMP = 0.25
NEG = -1e30
STAT_ROWS = 8
PIECES = 2
FIRST = 4
VMEM_LIMIT = 16 << 20
f32 = jnp.float32
bf16 = jnp.bfloat16


def core_of():
    return lax.axis_index("date") % 2


def chip_of():
    return lax.axis_index("date") // 2


def in_hbm(x):
    return pltpu.with_memory_space_constraint(x, pltpu.HBM)


def call(body, outs, *operands, scratch=(), flops=0, unread=0, place=()):
    whole = pl.BlockSpec(memory_space=pltpu.VMEM)
    anywhere = pl.BlockSpec(memory_space=pl.ANY)
    read = len(operands) - unread

    def kernel(*refs):
        body(*refs[:read], *refs[read + unread :])

    specs = [pl.BlockSpec(memory_space=p) for p in place]
    return pl.pallas_call(
        kernel,
        out_shape=[jax.ShapeDtypeStruct(*o) for o in outs],
        in_specs=specs + [whole] * (read - len(specs)) + [anywhere] * unread,
        out_specs=[whole] * len(outs),
        scratch_shapes=list(scratch),
        compiler_params=pltpu.CompilerParams(vmem_limit_bytes=VMEM_LIMIT),
        cost_estimate=pl.CostEstimate(flops=flops, bytes_accessed=0, transcendentals=0),
    )(*operands)


def log_add(a, b):
    return jnp.maximum(a, b) + jnp.log(1.0 + jnp.exp(-jnp.abs(a - b)))


def fill(out, inc, pay, may):
    dates = inc.shape[0]
    out[0:dates] = INVERSE_TEMP * inc
    for d in range(dates):
        out[dates + d] = jnp.where(may[d : d + 1, :] > 0, INVERSE_TEMP * pay[d], NEG)


def theirs_body(features, coefficients, payoff, exercise, send, held, weights, pay, may, sems, others):
    dates, paths, width = features.shape
    half, step = paths // 2, width // PIECES
    rows = pl.ds(pl.multiple_of((1 - core_of()) * half, half), half)
    parts = [slice(i * step, (i + 1) * step) for i in range(PIECES)]
    copies = [
        (
            pltpu.make_async_copy(features.at[:, rows, at], held.at[:, :, at], sems.at[2 * i]),
            pltpu.make_async_copy(coefficients.at[at, :], weights.at[at, :], sems.at[2 * i + 1]),
        )
        for i, at in enumerate(parts)
    ]
    small = (
        pltpu.make_async_copy(payoff.at[:, rows, :], pay, others.at[0]),
        pltpu.make_async_copy(exercise, may, others.at[1]),
    )
    for c in (*(c for pair in copies for c in pair), *small):
        c.start()
    inc = None
    for pair, at in zip(copies, parts):
        for c in pair:
            c.wait()
        left = held[:, :, at].reshape(dates * half, step)
        part = jnp.dot(left, weights[at, :], preferred_element_type=f32)
        inc = part if inc is None else inc + part
    for c in small:
        c.wait()
    fill(send, inc.reshape(dates, half, -1), pay, may)


def mine_body(features, payoff, exercise, weights, theirs, keep, held, pay, may, sems):
    dates, paths, width = features.shape
    half = paths // 2
    rows = pl.ds(pl.multiple_of(core_of() * half, half), half)
    copies = (
        pltpu.make_async_copy(features.at[:, rows, :], held.at[:, rows, :], sems.at[0]),
        pltpu.make_async_copy(payoff.at[:, rows, :], pay, sems.at[1]),
        pltpu.make_async_copy(exercise, may, sems.at[2]),
    )
    for c in copies:
        c.start()
    held[:, pl.ds(pl.multiple_of((1 - core_of()) * half, half), half), :] = theirs[...]
    for c in copies:
        c.wait()
    inc = jnp.dot(held[:, rows, :].reshape(dates * half, width), weights[...], preferred_element_type=f32)
    fill(keep, inc.reshape(dates, half, -1), pay, may)


def message_of(level, total, left, last):
    if last:
        return [jnp.where(left, level + total, level)]
    return [level, total]


def local_body(rounds, keep, other, score, level, total, message):
    dates = keep.shape[0] // 2
    first = core_of() == 0
    run = jnp.zeros(keep.shape[1:], f32)
    scores = []
    for part in (0, 1):
        for d in range(dates):
            inc, base = (
                jnp.where(first == (part == 0), keep[at], other[at]) for at in (d, dates + d)
            )
            run = run + inc
            scores.append(base - run)
    peak = functools.reduce(jnp.maximum, scores)
    lev = peak + jnp.log(sum(jnp.exp(s - peak) for s in scores))
    for i, s in enumerate(scores):
        score[i] = s
    level[...] = lev
    total[...] = run
    left = chip_of() % 2 == 0
    if rounds == 2:
        message[0] = jnp.where(left, lev + run, lev)
        return
    for i, m in enumerate(message_of(lev, run, left, rounds == 1)):
        message[i] = m


def pair_body(total, message, near, out):
    both = log_add(message[0], near[0])
    own = total[...]
    out[0] = both + jnp.where(chip_of() == 1, own, jnp.where(chip_of() == 2, -own, 0.0))


def merge_body(step, rounds, level, total, state, got, state2, message, *group):
    left = (chip_of() >> step) % 2 == 0
    lev, tot, other_lev, other_tot = level[...], total[...], got[0], got[1]
    if state is None:
        zero = jnp.zeros_like(lev)
        before, after, sum_before, sum_after = zero + NEG, zero + NEG, zero, zero
    else:
        before, after, sum_before, sum_after = (state[i] for i in range(4))
    state2[0] = jnp.where(left, before, log_add(before, other_lev + other_tot + sum_before))
    state2[1] = jnp.where(left, log_add(after, other_lev - sum_after), after)
    state2[2] = jnp.where(left, sum_before, sum_before + other_tot)
    state2[3] = jnp.where(left, sum_after + other_tot, sum_after)
    first_lev, first_tot = jnp.where(left, lev, other_lev), jnp.where(left, tot, other_tot)
    second_lev = jnp.where(left, other_lev, lev)
    lev2 = log_add(first_lev, second_lev - first_tot)
    tot2 = tot + other_tot
    for out, value in zip(group, (lev2, tot2)):
        out[...] = value
    next_left = (chip_of() >> (step + 1)) % 2 == 0
    for i, m in enumerate(message_of(lev2, tot2, next_left, step + 2 == rounds)):
        message[i] = m


def joined(rounds, state, got, zero):
    if state is None:
        before, after, sum_before, sum_after = zero + NEG, zero + NEG, zero, zero
    else:
        before, after, sum_before, sum_after = (state[i] for i in range(4))
    if got is not None:
        left = (chip_of() >> (rounds - 1)) % 2 == 0
        other = got[0]
        before = jnp.where(left, before, log_add(before, other + sum_before))
        after = jnp.where(left, log_add(after, other - sum_after), after)
    return before, after, sum_before


def joined_four(near, far, beside, across):
    first, left = chip_of() % 2 == 0, chip_of() < 2
    shift = jnp.where(first == left, beside[...], across[...])
    near, far = near[0], far[0] + jnp.where(left, -shift, shift)
    both, none = log_add(near, far), jnp.zeros_like(near) + NEG
    before = jnp.where(left, jnp.where(first, none, near), jnp.where(first, far, both))
    after = jnp.where(left, jnp.where(first, both, far), jnp.where(first, near, none))
    return before, after, jnp.where(first, 0.0, beside[...])


def tail_body(join, score, level, total, *refs):
    *given, out = refs
    lev, tot = level[...], total[...]
    before, after, sum_before = join(*given, jnp.zeros_like(lev))
    later = after - tot
    norm = log_add(log_add(before, lev), later)
    run = jnp.exp(later - norm)
    half = score.shape[1]
    for i in reversed(range(score.shape[0])):
        run = run + jnp.exp(score[i] - norm)
        out[i * half : (i + 1) * half, :] = run.astype(bf16).astype(f32)
    smoothed = TEMP * (norm - sum_before)
    at = score.shape[0] * half
    out[at : at + STAT_ROWS, :] = jnp.zeros((STAT_ROWS, smoothed.shape[1]), f32)
    out[at : at + 1, :] = jnp.sum(smoothed, axis=0, keepdims=True)
    out[at + 1 : at + 2, :] = jnp.sum(smoothed * smoothed, axis=0, keepdims=True)


def halves_body(chips, features, send):
    width = features.shape[2] // (2 * chips)
    for z in range(chips):
        at = pl.multiple_of((2 * z + 1 - core_of()) * width, width)
        send[:, :, z * width : (z + 1) * width] = features[:, :, pl.ds(at, width)].astype(f32)


def columns_body(chips, features, got, columns):
    dates, paths, whole = features.shape
    half, width = paths // 2, whole // (2 * chips)
    size = dates * half
    for z in range(chips):
        at = pl.multiple_of((2 * z + core_of()) * width, width)
        rows = slice(z * width, (z + 1) * width)
        for h in range(2):
            span = slice(h * half, (h + 1) * half)
            own = features[:, span, pl.ds(at, width)].reshape(size, width).T
            columns[rows, pl.ds(pl.multiple_of((2 * h + core_of()) * size, size), size)] = own
            other = got[:, span, rows].astype(bf16).reshape(size, width).T
            columns[rows, pl.ds(pl.multiple_of((2 * h + 1 - core_of()) * size, size), size)] = other


def side(columns, rows, half):
    size = columns.shape[1] // 2
    return columns[rows, pl.ds(pl.multiple_of(half * size, size), size)]


def first_body(scale, columns, own, out):
    size = columns.shape[1] // 2
    right = own[:size, :].astype(bf16)
    step = columns.shape[0] // FIRST
    for i in range(FIRST):
        rows = slice(i * step, (i + 1) * step)
        out[rows, :] = scale * jnp.dot(side(columns, rows, core_of()), right, preferred_element_type=f32)


def product_body(scale, far, near, columns, begun, own, got, *refs):
    keep, message, *outs, product = refs
    size = columns.shape[1] // 2
    right = got[:size, :].astype(bf16)
    chips, count, rows, contracts = product.shape
    width = count * rows
    for z in range(chips):
        at = slice(z * width, (z + 1) * width)
        block = scale * jnp.dot(side(columns, at, 1 - core_of()), right, preferred_element_type=f32)
        product[z] = (begun[at, :] + block).reshape(count, rows, contracts)
    stats = own[size:, :] + got[size:, :]
    halve(0, product, [partner(chip_of(), j, chips) for j in far], stats, keep, message)
    for j, out in zip(near, outs):
        out[...] = product[partner(chip_of(), j, chips)].reshape(out.shape)


def path_bits(count):
    bits = list(range(count.bit_length() - 1))
    return bits, bits[len(bits) // 2 :] + bits[: len(bits) // 2]


def halve(step, product, chosen, stats, keep, message):
    _, n, rows, _ = product.shape
    first, second = path_bits(lax.axis_size("path"))
    bit, place = (
        jnp.where(core_of() == 0, a, b)
        for a, b in (
            (first[step], second[step]),
            tuple(sum(x < order[step] for x in order[step + 1 :]) for order in (first, second)),
        )
    )
    mine = (lax.axis_index("path") >> bit) & 1
    for out, value in ((keep, mine), (message, 1 - mine)):
        for k, z in enumerate(chosen):
            for i in range(n // 2):
                low = i & ((1 << place) - 1)
                at = ((i - low) << 1) + (value << place) + low
                start = (k * (n // 2) + i) * rows
                out[start : start + rows, :] = product[z, at]
        if stats is not None:
            out[len(chosen) * (n // 2) * rows :, :] = stats


def path_pairs(chips, count, step):
    first, second = path_bits(count)
    return [
        ((2 * z + core) * count + p, (2 * z + core) * count + (p ^ (1 << order[step])))
        for z in range(chips)
        for core, order in enumerate((first, second))
        for p in range(count)
    ]


def path_sum_body(step, *refs):
    *given, keep, message, product = refs
    chips, n, rows, _ = product.shape
    size = chips * n * rows
    total = functools.reduce(lambda a, b: a + b, (p[...] for p in given))
    product[...] = total[:size, :].reshape(product.shape)
    halve(step, product, range(chips), total[size:, :] if total.shape[0] > size else None, keep, message)


def partner(me, j, count):
    if count & (count - 1) == 0:
        return me ^ j
    return lax.rem(me + j, count)


def pairs(count, j):
    if count & (count - 1) == 0:
        return [(i, i ^ j) for i in range(count)]
    return [(i, (i + j) % count) for i in range(count)]


def date_pairs(chips, j):
    return [(2 * a + core, 2 * b + core) for a, b in pairs(chips, j) for core in range(2)]


def inner_pairs():
    inner = [(2 * a + c, 6 - 2 * a + c) for a in (1, 2) for c in range(2)]
    return inner + [(2 * a + c, 2 * a + 1 - c) for a in (0, 3) for c in range(2)]


def part_sum_body(chips, rows, mine, got, *outs):
    total = mine[...] + got[...]
    for k, out in enumerate(outs[:chips]):
        out[0:rows, :] = total[k * rows : (k + 1) * rows, :]
        if out.shape[0] > rows:
            out[rows:, :] = total[chips * rows :, :]
    for out in outs[chips:]:
        out[...] = total[chips * rows :, :]


def date_sum_body(chips, paths_total, stats, across, *refs):
    parts, (gradient, bound, spread) = refs[:-3], refs[-3:]
    rows = gradient.shape[0]
    gradient[...] = functools.reduce(lambda a, b: a + b, (p[:rows, :] for p in parts), across[:rows, :])
    sums = jnp.where(chip_of() < chips // 2, stats[...], across[rows:, :])
    mean = sums[0:1, :] * (1.0 / paths_total)
    bound[...] = mean
    spread[...] = sums[1:2, :] * (1.0 / paths_total) - mean * mean


def chip_order(chips):
    return sorted(range(1, chips), key=lambda j: (-j.bit_length(), j))


def shards(features, payoff, coefficients, exercise):
    dates, paths, width = features.shape
    contracts = coefficients.shape[1]
    chips, count = lax.axis_size("date") // 2, lax.axis_size("path")
    rounds = chips.bit_length() - 1
    assert chips == 1 << rounds
    half, paths_total = paths // 2, paths * count
    rows = width // (2 * chips * count)
    cores = [(2 * z + c, 2 * z + 1 - c) for z in range(chips) for c in range(2)]
    plane = (half, contracts)

    halves = (dates, half, width)
    send, theirs, weights = call(
        theirs_body,
        [((2 * dates, *plane), f32), (halves, bf16), (coefficients.shape, bf16)],
        *(in_hbm(x) for x in (features, coefficients, payoff, exercise)),
        scratch=[
            pltpu.VMEM((dates, half, contracts), f32),
            pltpu.VMEM(exercise.shape, jnp.int32),
            pltpu.SemaphoreType.DMA((2 * PIECES,)),
            pltpu.SemaphoreType.DMA((2,)),
        ],
        place=[pltpu.HBM] * 4,
    )
    other = lax.ppermute(send, "date", cores)
    keep, held = call(
        mine_body,
        [((2 * dates, *plane), f32), (features.shape, bf16)],
        *(in_hbm(x) for x in (features, payoff, exercise)),
        weights,
        theirs,
        scratch=[
            pltpu.VMEM((dates, half, contracts), f32),
            pltpu.VMEM(exercise.shape, jnp.int32),
            pltpu.SemaphoreType.DMA((3,)),
        ],
        place=[pltpu.HBM] * 3,
    )
    sizes = [1 if step + 1 == rounds or rounds == 2 else 2 for step in range(rounds)] or [2]
    score, level, total, message = call(
        functools.partial(local_body, rounds),
        [((2 * dates, *plane), f32), (plane, f32), (plane, f32), ((sizes[0], *plane), f32)],
        keep,
        other,
    )
    (columns_send,) = call(
        functools.partial(halves_body, chips),
        [((dates, paths, width // 2), f32)],
        held,
        message,
        unread=1,
    )
    columns_got = lax.ppermute(columns_send, "date", cores)
    own_level, own_total, state, got = level, total, None, None
    if rounds == 2:
        near = lax.ppermute(message, "date", date_pairs(chips, 1))
        beside = lax.ppermute(total, "date", date_pairs(chips, 1))
        across = lax.ppermute(total, "date", inner_pairs())
        (message,) = call(pair_body, [((1, *plane), f32)], total, message, near)
        far = lax.ppermute(message, "date", date_pairs(chips, 2))
        given, turn = [near, far, beside, across], [beside, across]
        join = lambda *refs: joined_four(*refs[:4])
    else:
        for step in range(rounds):
            got = lax.ppermute(message, "date", date_pairs(chips, 1 << step))
            if step + 1 == rounds:
                break
            body = functools.partial(merge_body, step, rounds)
            if state is None:
                body = lambda a, b, c, *o, body=body: body(a, b, None, c, *o)
            operands = [level, total, got] if state is None else [level, total, state, got]
            group = [(plane, f32)] * (0 if step + 2 == rounds else 2)
            state, message, *group = call(
                body, [((4, *plane), f32), ((sizes[step + 1], *plane), f32)] + group, *operands
            )
            level, total = group or (level, total)
        given, turn = [x for x in (state, got) if x is not None], [message]

        def join(*refs, joined=joined):
            *refs, zero = refs
            held = refs[0] if state is not None else None
            return joined(rounds, held, refs[-1] if got is not None else None, zero)

    (columns,) = call(
        functools.partial(columns_body, chips),
        [((width // 2, 2 * dates * paths), bf16)],
        held,
        columns_got,
        *turn,
        unread=len(turn),
        flops=1 << 27,
    )
    (tail,) = call(
        functools.partial(tail_body, join),
        [((2 * dates * half + STAT_ROWS, contracts), f32)],
        score,
        own_level,
        own_total,
        *given,
        columns,
        unread=1,
    )
    tail_other = lax.ppermute(tail, "date", cores)
    steps = count.bit_length() - 1
    assert count == 1 << steps and steps > 0
    near, far = list(range(chips // 2)), list(range(chips // 2, chips))

    def piece(n, chips, stats=False):
        return ((chips * n * rows + (STAT_ROWS if stats else 0), contracts), f32)

    def over_path(step, message):
        return lax.ppermute(message, ("date", "path"), path_pairs(chips, count, step))

    def over_date(j, message):
        return lax.ppermute(message, "date", date_pairs(chips, j))

    def next_round(step, given, after, chips, stats):
        n = count >> step
        return call(
            functools.partial(path_sum_body, step),
            [piece(n // 2, chips, stats)] * 2,
            *given,
            *after,
            unread=len(after),
            scratch=[pltpu.VMEM((chips, n, rows, contracts), f32)],
        )

    (begun,) = call(
        functools.partial(first_body, -1.0 / paths_total),
        [((width // 2, contracts), f32)],
        columns,
        tail,
        flops=dates * paths * width * contracts,
    )
    keep, message, *firsts = call(
        functools.partial(product_body, -1.0 / paths_total, far, near),
        [piece(count // 2, len(far), True)] * 2 + [piece(count, 1)] * len(near),
        columns,
        begun,
        tail,
        tail_other,
        scratch=[pltpu.VMEM((chips, count, rows, contracts), f32)],
        flops=dates * paths * width * contracts,
    )
    got = over_path(0, message)
    near_parts = [firsts[0]] + [over_date(j, firsts[j]) for j in chip_order(chips) if j in near]
    for step in range(1, steps):
        keep, message = next_round(step, [keep, got], [], len(far), True)
        got = over_path(step, message)
        near_keep, near_message = next_round(step - 1, near_parts, [message], 1, False)
        near_parts = [near_keep, over_path(step - 1, near_message)]
    row = ((rows, contracts), f32)
    *sums, stats = call(
        functools.partial(part_sum_body, len(far), rows),
        [piece(1, 1, True)] * len(far) + [((STAT_ROWS, contracts), f32)],
        keep,
        got,
        *([near_message] if steps > 1 else []),
        unread=min(1, steps - 1),
    )
    over = [over_date(j, sums[far.index(j)]) for j in chip_order(chips) if j in far]
    near_keep, near_message = next_round(steps - 1, near_parts, sums[:1], 1, False)
    over += [near_keep, over_path(steps - 1, near_message)]
    gradient, bound, spread = call(
        functools.partial(date_sum_body, chips, paths_total),
        [row, ((1, contracts), f32), ((1, contracts), f32)],
        stats,
        *over,
    )
    return gradient, bound.reshape(contracts), spread.reshape(contracts)


def solution(mesh):
    placed = (P("date", "path", None), P("date", "path", None), P(), P("date", None))
    return jax.shard_map(
        shards,
        mesh=mesh,
        in_specs=placed,
        out_specs=(P(("date", "path"), None), P(), P()),
        check_vma=False,
    )
```

```python
import functools

import jax
import jax.numpy as jnp
from jax import lax
from jax.experimental import pallas as pl
from jax.experimental.pallas import tpu as pltpu
from jax.sharding import PartitionSpec as P

INVERSE_TEMP = 4.0
TEMP = 0.25
NEG = -1e30
STAT_ROWS = 8
PIECES = 2
FIRST = 4
VMEM_LIMIT = 16 << 20
f32 = jnp.float32
bf16 = jnp.bfloat16


def core_of():
    return lax.axis_index("date") % 2


def chip_of():
    return lax.axis_index("date") // 2


def in_hbm(x):
    return pltpu.with_memory_space_constraint(x, pltpu.HBM)


def call(body, outs, *operands, scratch=(), flops=0, unread=0, place=()):
    whole = pl.BlockSpec(memory_space=pltpu.VMEM)
    anywhere = pl.BlockSpec(memory_space=pl.ANY)
    read = len(operands) - unread

    def kernel(*refs):
        body(*refs[:read], *refs[read + unread :])

    specs = [pl.BlockSpec(memory_space=p) for p in place]
    return pl.pallas_call(
        kernel,
        out_shape=[jax.ShapeDtypeStruct(*o) for o in outs],
        in_specs=specs + [whole] * (read - len(specs)) + [anywhere] * unread,
        out_specs=[whole] * len(outs),
        scratch_shapes=list(scratch),
        compiler_params=pltpu.CompilerParams(vmem_limit_bytes=VMEM_LIMIT),
        cost_estimate=pl.CostEstimate(flops=flops, bytes_accessed=0, transcendentals=0),
    )(*operands)


def log_add(a, b):
    return jnp.maximum(a, b) + jnp.log(1.0 + jnp.exp(-jnp.abs(a - b)))


def fill(out, inc, pay, may):
    dates = inc.shape[0]
    out[0:dates] = INVERSE_TEMP * inc
    for d in range(dates):
        out[dates + d] = jnp.where(may[d : d + 1, :] > 0, INVERSE_TEMP * pay[d], NEG)


def theirs_body(features, coefficients, payoff, exercise, send, held, weights, pay, may, sems, others):
    dates, paths, width = features.shape
    half, step = paths // 2, width // PIECES
    rows = pl.ds(pl.multiple_of((1 - core_of()) * half, half), half)
    parts = [slice(i * step, (i + 1) * step) for i in range(PIECES)]
    copies = [
        (
            pltpu.make_async_copy(features.at[:, rows, at], held.at[:, :, at], sems.at[2 * i]),
            pltpu.make_async_copy(coefficients.at[at, :], weights.at[at, :], sems.at[2 * i + 1]),
        )
        for i, at in enumerate(parts)
    ]
    small = (
        pltpu.make_async_copy(payoff.at[:, rows, :], pay, others.at[0]),
        pltpu.make_async_copy(exercise, may, others.at[1]),
    )
    for c in (*(c for pair in copies for c in pair), *small):
        c.start()
    inc = None
    for pair, at in zip(copies, parts):
        for c in pair:
            c.wait()
        left = held[:, :, at].reshape(dates * half, step)
        part = jnp.dot(left, weights[at, :], preferred_element_type=f32)
        inc = part if inc is None else inc + part
    for c in small:
        c.wait()
    fill(send, inc.reshape(dates, half, -1), pay, may)


def mine_body(features, payoff, exercise, weights, theirs, keep, held, pay, may, sems):
    dates, paths, width = features.shape
    half = paths // 2
    rows = pl.ds(pl.multiple_of(core_of() * half, half), half)
    copies = (
        pltpu.make_async_copy(features.at[:, rows, :], held.at[:, rows, :], sems.at[0]),
        pltpu.make_async_copy(payoff.at[:, rows, :], pay, sems.at[1]),
        pltpu.make_async_copy(exercise, may, sems.at[2]),
    )
    for c in copies:
        c.start()
    held[:, pl.ds(pl.multiple_of((1 - core_of()) * half, half), half), :] = theirs[...]
    for c in copies:
        c.wait()
    inc = jnp.dot(held[:, rows, :].reshape(dates * half, width), weights[...], preferred_element_type=f32)
    fill(keep, inc.reshape(dates, half, -1), pay, may)


def message_of(level, total, left, last):
    if last:
        return [jnp.where(left, level + total, level)]
    return [level, total]


def local_body(rounds, keep, other, score, level, total, message):
    dates = keep.shape[0] // 2
    first = core_of() == 0
    run = jnp.zeros(keep.shape[1:], f32)
    scores = []
    for part in (0, 1):
        for d in range(dates):
            inc, base = (
                jnp.where(first == (part == 0), keep[at], other[at]) for at in (d, dates + d)
            )
            run = run + inc
            scores.append(base - run)
    peak = functools.reduce(jnp.maximum, scores)
    lev = peak + jnp.log(sum(jnp.exp(s - peak) for s in scores))
    for i, s in enumerate(scores):
        score[i] = s
    level[...] = lev
    total[...] = run
    left = chip_of() % 2 == 0
    if rounds == 2:
        message[0] = jnp.where(left, lev + run, lev)
        return
    for i, m in enumerate(message_of(lev, run, left, rounds == 1)):
        message[i] = m


def pair_body(total, message, near, out):
    both = log_add(message[0], near[0])
    own = total[...]
    out[0] = both + jnp.where(chip_of() == 1, own, jnp.where(chip_of() == 2, -own, 0.0))


def merge_body(step, rounds, level, total, state, got, state2, message, *group):
    left = (chip_of() >> step) % 2 == 0
    lev, tot, other_lev, other_tot = level[...], total[...], got[0], got[1]
    if state is None:
        zero = jnp.zeros_like(lev)
        before, after, sum_before, sum_after = zero + NEG, zero + NEG, zero, zero
    else:
        before, after, sum_before, sum_after = (state[i] for i in range(4))
    state2[0] = jnp.where(left, before, log_add(before, other_lev + other_tot + sum_before))
    state2[1] = jnp.where(left, log_add(after, other_lev - sum_after), after)
    state2[2] = jnp.where(left, sum_before, sum_before + other_tot)
    state2[3] = jnp.where(left, sum_after + other_tot, sum_after)
    first_lev, first_tot = jnp.where(left, lev, other_lev), jnp.where(left, tot, other_tot)
    second_lev = jnp.where(left, other_lev, lev)
    lev2 = log_add(first_lev, second_lev - first_tot)
    tot2 = tot + other_tot
    for out, value in zip(group, (lev2, tot2)):
        out[...] = value
    next_left = (chip_of() >> (step + 1)) % 2 == 0
    for i, m in enumerate(message_of(lev2, tot2, next_left, step + 2 == rounds)):
        message[i] = m


def joined(rounds, state, got, zero):
    if state is None:
        before, after, sum_before, sum_after = zero + NEG, zero + NEG, zero, zero
    else:
        before, after, sum_before, sum_after = (state[i] for i in range(4))
    if got is not None:
        left = (chip_of() >> (rounds - 1)) % 2 == 0
        other = got[0]
        before = jnp.where(left, before, log_add(before, other + sum_before))
        after = jnp.where(left, log_add(after, other - sum_after), after)
    return before, after, sum_before


def joined_four(near, far, beside, across):
    first, left = chip_of() % 2 == 0, chip_of() < 2
    shift = jnp.where(first == left, beside[...], across[...])
    near, far = near[0], far[0] + jnp.where(left, -shift, shift)
    both, none = log_add(near, far), jnp.zeros_like(near) + NEG
    before = jnp.where(left, jnp.where(first, none, near), jnp.where(first, far, both))
    after = jnp.where(left, jnp.where(first, both, far), jnp.where(first, near, none))
    return before, after, jnp.where(first, 0.0, beside[...])


def tail_body(join, score, level, total, *refs):
    *given, out = refs
    lev, tot = level[...], total[...]
    before, after, sum_before = join(*given, jnp.zeros_like(lev))
    later = after - tot
    norm = log_add(log_add(before, lev), later)
    run = jnp.exp(later - norm)
    half = score.shape[1]
    for i in reversed(range(score.shape[0])):
        run = run + jnp.exp(score[i] - norm)
        out[i * half : (i + 1) * half, :] = run.astype(bf16).astype(f32)
    smoothed = TEMP * (norm - sum_before)
    at = score.shape[0] * half
    out[at : at + STAT_ROWS, :] = jnp.zeros((STAT_ROWS, smoothed.shape[1]), f32)
    out[at : at + 1, :] = jnp.sum(smoothed, axis=0, keepdims=True)
    out[at + 1 : at + 2, :] = jnp.sum(smoothed * smoothed, axis=0, keepdims=True)


def halves_body(chips, features, send):
    width = features.shape[2] // (2 * chips)
    for z in range(chips):
        at = pl.multiple_of((2 * z + 1 - core_of()) * width, width)
        send[:, :, z * width : (z + 1) * width] = features[:, :, pl.ds(at, width)].astype(f32)


def columns_body(chips, features, got, columns):
    dates, paths, whole = features.shape
    half, width = paths // 2, whole // (2 * chips)
    size = dates * half
    for z in range(chips):
        at = pl.multiple_of((2 * z + core_of()) * width, width)
        rows = slice(z * width, (z + 1) * width)
        for h in range(2):
            span = slice(h * half, (h + 1) * half)
            own = features[:, span, pl.ds(at, width)].reshape(size, width).T
            columns[rows, pl.ds(pl.multiple_of((2 * h + core_of()) * size, size), size)] = own
            other = got[:, span, rows].astype(bf16).reshape(size, width).T
            columns[rows, pl.ds(pl.multiple_of((2 * h + 1 - core_of()) * size, size), size)] = other


def side(columns, rows, half):
    size = columns.shape[1] // 2
    return columns[rows, pl.ds(pl.multiple_of(half * size, size), size)]


def first_body(scale, columns, own, out):
    size = columns.shape[1] // 2
    right = own[:size, :].astype(bf16)
    step = columns.shape[0] // FIRST
    for i in range(FIRST):
        rows = slice(i * step, (i + 1) * step)
        out[rows, :] = scale * jnp.dot(side(columns, rows, core_of()), right, preferred_element_type=f32)


def rows_of(scale, j, width, columns, begun, right):
    chip = partner(chip_of(), j, begun.shape[0] // width)
    at = pl.ds(pl.multiple_of(chip * width, width), width)
    return begun[at, :] + scale * jnp.dot(side(columns, at, 1 - core_of()), right, preferred_element_type=f32)


def far_body(scale, far, columns, begun, own, got, keep, message, product):
    size = columns.shape[1] // 2
    right = got[:size, :].astype(bf16)
    _, count, rows, _ = product.shape
    for k, j in enumerate(far):
        product[k] = rows_of(scale, j, count * rows, columns, begun, right).reshape(product.shape[1:])
    halve(0, product, own[size:, :] + got[size:, :], keep, message)


def near_body(scale, near, columns, begun, got, *outs):
    right = got[: columns.shape[1] // 2, :].astype(bf16)
    for j, out in zip(near, outs):
        out[...] = rows_of(scale, j, out.shape[0], columns, begun, right)


def path_bits(count):
    bits = list(range(count.bit_length() - 1))
    return bits, bits[len(bits) // 2 :] + bits[: len(bits) // 2]


def halve(step, product, stats, keep, message):
    chips, n, rows, _ = product.shape
    first, second = path_bits(lax.axis_size("path"))
    bit, place = (
        jnp.where(core_of() == 0, a, b)
        for a, b in (
            (first[step], second[step]),
            tuple(sum(x < order[step] for x in order[step + 1 :]) for order in (first, second)),
        )
    )
    mine = (lax.axis_index("path") >> bit) & 1
    for out, value in ((keep, mine), (message, 1 - mine)):
        start = 0
        for k in range(chips):
            for i in range(n // 2):
                low = i & ((1 << place) - 1)
                out[start : start + rows, :] = product[k, ((i - low) << 1) + (value << place) + low]
                start += rows
        if stats is not None:
            out[start:, :] = stats


def path_pairs(chips, count, step):
    first, second = path_bits(count)
    return [
        ((2 * z + core) * count + p, (2 * z + core) * count + (p ^ (1 << order[step])))
        for z in range(chips)
        for core, order in enumerate((first, second))
        for p in range(count)
    ]


def path_sum_body(step, *refs):
    *given, keep, message, product = refs
    size = product.shape[0] * product.shape[1] * product.shape[2]
    total = functools.reduce(lambda a, b: a + b, (p[...] for p in given))
    product[...] = total[:size, :].reshape(product.shape)
    halve(step, product, total[size:, :] if total.shape[0] > size else None, keep, message)


def partner(me, j, count):
    if count & (count - 1) == 0:
        return me ^ j
    return lax.rem(me + j, count)


def pairs(count, j):
    if count & (count - 1) == 0:
        return [(i, i ^ j) for i in range(count)]
    return [(i, (i + j) % count) for i in range(count)]


def date_pairs(chips, j):
    return [(2 * a + core, 2 * b + core) for a, b in pairs(chips, j) for core in range(2)]


def inner_pairs():
    inner = [(2 * a + c, 6 - 2 * a + c) for a in (1, 2) for c in range(2)]
    return inner + [(2 * a + c, 2 * a + 1 - c) for a in (0, 3) for c in range(2)]


def part_sum_body(rows, mine, got, *outs):
    total = mine[...] + got[...]
    chips = len(outs) - 1
    blocks = [total[k * rows : (k + 1) * rows, :] for k in range(chips)]
    for first, second, out in zip(blocks, blocks[::-1], outs):
        out[0:rows, :] = jnp.where(core_of() == 0, first, second)
        out[rows:, :] = total[chips * rows :, :]
    outs[-1][...] = total[chips * rows :, :]


def date_sum_body(chips, paths_total, stats, across, *refs):
    parts, (gradient, bound, spread) = refs[:-3], refs[-3:]
    rows = gradient.shape[0]
    gradient[...] = functools.reduce(lambda a, b: a + b, (p[:rows, :] for p in parts), across[:rows, :])
    sums = jnp.where(chip_of() < chips // 2, stats[...], across[rows:, :])
    mean = sums[0:1, :] * (1.0 / paths_total)
    bound[...] = mean
    spread[...] = sums[1:2, :] * (1.0 / paths_total) - mean * mean


def far_pairs(chips, far, k):
    return [(2 * z + c, 2 * (z ^ (far, far[::-1])[c][k]) + c) for z in range(chips) for c in range(2)]


def shards(features, payoff, coefficients, exercise):
    dates, paths, width = features.shape
    contracts = coefficients.shape[1]
    chips, count = lax.axis_size("date") // 2, lax.axis_size("path")
    rounds = chips.bit_length() - 1
    assert chips == 1 << rounds
    half, paths_total = paths // 2, paths * count
    rows = width // (2 * chips * count)
    cores = [(2 * z + c, 2 * z + 1 - c) for z in range(chips) for c in range(2)]
    plane = (half, contracts)

    halves = (dates, half, width)
    send, theirs, weights = call(
        theirs_body,
        [((2 * dates, *plane), f32), (halves, bf16), (coefficients.shape, bf16)],
        *(in_hbm(x) for x in (features, coefficients, payoff, exercise)),
        scratch=[
            pltpu.VMEM((dates, half, contracts), f32),
            pltpu.VMEM(exercise.shape, jnp.int32),
            pltpu.SemaphoreType.DMA((2 * PIECES,)),
            pltpu.SemaphoreType.DMA((2,)),
        ],
        place=[pltpu.HBM] * 4,
    )
    other = lax.ppermute(send, "date", cores)
    keep, held = call(
        mine_body,
        [((2 * dates, *plane), f32), (features.shape, bf16)],
        *(in_hbm(x) for x in (features, payoff, exercise)),
        weights,
        theirs,
        scratch=[
            pltpu.VMEM((dates, half, contracts), f32),
            pltpu.VMEM(exercise.shape, jnp.int32),
            pltpu.SemaphoreType.DMA((3,)),
        ],
        place=[pltpu.HBM] * 3,
    )
    sizes = [1 if step + 1 == rounds or rounds == 2 else 2 for step in range(rounds)] or [2]
    score, level, total, message = call(
        functools.partial(local_body, rounds),
        [((2 * dates, *plane), f32), (plane, f32), (plane, f32), ((sizes[0], *plane), f32)],
        keep,
        other,
    )
    (columns_send,) = call(
        functools.partial(halves_body, chips),
        [((dates, paths, width // 2), f32)],
        held,
        message,
        unread=1,
    )
    columns_got = lax.ppermute(columns_send, "date", cores)
    own_level, own_total, state, got = level, total, None, None
    if rounds == 2:
        near = lax.ppermute(message, "date", date_pairs(chips, 1))
        beside = lax.ppermute(total, "date", date_pairs(chips, 1))
        across = lax.ppermute(total, "date", inner_pairs())
        (message,) = call(pair_body, [((1, *plane), f32)], total, message, near)
        far = lax.ppermute(message, "date", date_pairs(chips, 2))
        given, turn = [near, far, beside, across], [beside, across]
        join = lambda *refs: joined_four(*refs[:4])
    else:
        for step in range(rounds):
            got = lax.ppermute(message, "date", date_pairs(chips, 1 << step))
            if step + 1 == rounds:
                break
            body = functools.partial(merge_body, step, rounds)
            if state is None:
                body = lambda a, b, c, *o, body=body: body(a, b, None, c, *o)
            operands = [level, total, got] if state is None else [level, total, state, got]
            group = [(plane, f32)] * (0 if step + 2 == rounds else 2)
            state, message, *group = call(
                body, [((4, *plane), f32), ((sizes[step + 1], *plane), f32)] + group, *operands
            )
            level, total = group or (level, total)
        given, turn = [x for x in (state, got) if x is not None], [message]

        def join(*refs, joined=joined):
            *refs, zero = refs
            held = refs[0] if state is not None else None
            return joined(rounds, held, refs[-1] if got is not None else None, zero)

    (columns,) = call(
        functools.partial(columns_body, chips),
        [((width // 2, 2 * dates * paths), bf16)],
        held,
        columns_got,
        *turn,
        unread=len(turn),
        flops=1 << 27,
    )
    (tail,) = call(
        functools.partial(tail_body, join),
        [((2 * dates * half + STAT_ROWS, contracts), f32)],
        score,
        own_level,
        own_total,
        *given,
        columns,
        unread=1,
    )
    tail_other = lax.ppermute(tail, "date", cores)
    steps = count.bit_length() - 1
    assert count == 1 << steps and steps > 0
    near, far = list(range(chips // 2)), list(range(chips // 2, chips))

    def piece(n, part, stats=False):
        return ((n * part * rows + (STAT_ROWS if stats else 0), contracts), f32)

    def over_path(step, message):
        return lax.ppermute(message, ("date", "path"), path_pairs(chips, count, step))

    def next_round(step, given, after, part, stats):
        n = count >> step
        return call(
            functools.partial(path_sum_body, step),
            [piece(n // 2, part, stats)] * 2,
            *given,
            *after,
            unread=len(after),
            scratch=[pltpu.VMEM((part, n, rows, contracts), f32)],
        )

    (begun,) = call(
        functools.partial(first_body, -1.0 / paths_total),
        [((width // 2, contracts), f32)],
        columns,
        tail,
        flops=dates * paths * width * contracts,
    )
    keep, message = call(
        functools.partial(far_body, -1.0 / paths_total, far),
        [piece(count // 2, len(far), True)] * 2,
        columns,
        begun,
        tail,
        tail_other,
        scratch=[pltpu.VMEM((len(far), count, rows, contracts), f32)],
        flops=dates * paths * width * contracts // 2,
    )
    got = over_path(0, message)
    firsts = call(
        functools.partial(near_body, -1.0 / paths_total, near),
        [piece(count, 1)] * len(near),
        columns,
        begun,
        tail_other,
        message,
        unread=1,
        flops=dates * paths * width * contracts // 2,
    )
    near_parts = [lax.ppermute(x, "date", date_pairs(chips, j)) if j else x for j, x in zip(near, firsts)]
    assert steps > 1
    for step in range(1, steps):
        keep, message = next_round(step, [keep, got], [], len(far), True)
        got = over_path(step, message)
        near_keep, near_message = next_round(step - 1, near_parts, [message], 1, False)
        near_parts = [near_keep, over_path(step - 1, near_message)]
    *sums, stats = call(
        functools.partial(part_sum_body, rows),
        [piece(1, 1, True)] * len(far) + [((STAT_ROWS, contracts), f32)],
        keep,
        got,
        near_message,
        unread=1,
    )
    over = [lax.ppermute(x, "date", far_pairs(chips, far, k)) for k, x in enumerate(sums)]
    near_keep, near_message = next_round(steps - 1, near_parts, sums[:1], 1, False)
    over += [near_keep, over_path(steps - 1, near_message)]
    gradient, bound, spread = call(
        functools.partial(date_sum_body, chips, paths_total),
        [((rows, contracts), f32), ((1, contracts), f32), ((1, contracts), f32)],
        stats,
        *over,
    )
    return gradient, bound.reshape(contracts), spread.reshape(contracts)


def solution(mesh):
    placed = (P("date", "path", None), P("date", "path", None), P(), P("date", None))
    return jax.shard_map(
        shards,
        mesh=mesh,
        in_specs=placed,
        out_specs=(P(("date", "path"), None), P(), P()),
        check_vma=False,
    )
```

```python
import functools

import jax
import jax.numpy as jnp
from jax import lax
from jax.experimental import pallas as pl
from jax.experimental.pallas import tpu as pltpu
from jax.sharding import PartitionSpec as P

INVERSE_TEMP = 4.0
TEMP = 0.25
NEG = -1e30
STAT_ROWS = 8
PIECES = 2
FIRST = 4
VMEM_LIMIT = 16 << 20
f32 = jnp.float32
bf16 = jnp.bfloat16


def core_of():
    return lax.axis_index("date") % 2


def chip_of():
    return lax.axis_index("date") // 2


def in_hbm(x):
    return pltpu.with_memory_space_constraint(x, pltpu.HBM)


def call(body, outs, *operands, scratch=(), flops=0, unread=0, place=()):
    whole = pl.BlockSpec(memory_space=pltpu.VMEM)
    anywhere = pl.BlockSpec(memory_space=pl.ANY)
    read = len(operands) - unread

    def kernel(*refs):
        body(*refs[:read], *refs[read + unread :])

    specs = [pl.BlockSpec(memory_space=p) for p in place]
    return pl.pallas_call(
        kernel,
        out_shape=[jax.ShapeDtypeStruct(*o) for o in outs],
        in_specs=specs + [whole] * (read - len(specs)) + [anywhere] * unread,
        out_specs=[whole] * len(outs),
        scratch_shapes=list(scratch),
        compiler_params=pltpu.CompilerParams(vmem_limit_bytes=VMEM_LIMIT),
        cost_estimate=pl.CostEstimate(flops=flops, bytes_accessed=0, transcendentals=0),
    )(*operands)


def log_add(a, b):
    return jnp.maximum(a, b) + jnp.log(1.0 + jnp.exp(-jnp.abs(a - b)))


def fill(out, inc, pay, may):
    dates = inc.shape[0]
    out[0:dates] = INVERSE_TEMP * inc
    for d in range(dates):
        out[dates + d] = jnp.where(may[d : d + 1, :] > 0, INVERSE_TEMP * pay[d], NEG)


def theirs_body(features, coefficients, payoff, exercise, send, held, weights, pay, may, sems, others):
    dates, paths, width = features.shape
    half, step = paths // 2, width // PIECES
    rows = pl.ds(pl.multiple_of((1 - core_of()) * half, half), half)
    parts = [slice(i * step, (i + 1) * step) for i in range(PIECES)]
    copies = [
        (
            pltpu.make_async_copy(features.at[:, rows, at], held.at[:, :, at], sems.at[2 * i]),
            pltpu.make_async_copy(coefficients.at[at, :], weights.at[at, :], sems.at[2 * i + 1]),
        )
        for i, at in enumerate(parts)
    ]
    small = (
        pltpu.make_async_copy(payoff.at[:, rows, :], pay, others.at[0]),
        pltpu.make_async_copy(exercise, may, others.at[1]),
    )
    for c in (*(c for pair in copies for c in pair), *small):
        c.start()
    inc = None
    for pair, at in zip(copies, parts):
        for c in pair:
            c.wait()
        left = held[:, :, at].reshape(dates * half, step)
        part = jnp.dot(left, weights[at, :], preferred_element_type=f32)
        inc = part if inc is None else inc + part
    for c in small:
        c.wait()
    fill(send, inc.reshape(dates, half, -1), pay, may)


def mine_body(features, payoff, exercise, weights, theirs, keep, held, pay, may, sems):
    dates, paths, width = features.shape
    half = paths // 2
    rows = pl.ds(pl.multiple_of(core_of() * half, half), half)
    copies = (
        pltpu.make_async_copy(features.at[:, rows, :], held.at[:, rows, :], sems.at[0]),
        pltpu.make_async_copy(payoff.at[:, rows, :], pay, sems.at[1]),
        pltpu.make_async_copy(exercise, may, sems.at[2]),
    )
    for c in copies:
        c.start()
    held[:, pl.ds(pl.multiple_of((1 - core_of()) * half, half), half), :] = theirs[...]
    for c in copies:
        c.wait()
    inc = jnp.dot(held[:, rows, :].reshape(dates * half, width), weights[...], preferred_element_type=f32)
    fill(keep, inc.reshape(dates, half, -1), pay, may)


def message_of(level, total, left, last):
    if last:
        return [jnp.where(left, level + total, level)]
    return [level, total]


def local_body(rounds, keep, other, score, level, total, message):
    dates = keep.shape[0] // 2
    first = core_of() == 0
    run = jnp.zeros(keep.shape[1:], f32)
    scores = []
    for part in (0, 1):
        for d in range(dates):
            inc, base = (
                jnp.where(first == (part == 0), keep[at], other[at]) for at in (d, dates + d)
            )
            run = run + inc
            scores.append(base - run)
    peak = functools.reduce(jnp.maximum, scores)
    lev = peak + jnp.log(sum(jnp.exp(s - peak) for s in scores))
    for i, s in enumerate(scores):
        score[i] = s
    level[...] = lev
    total[...] = run
    left = chip_of() % 2 == 0
    if rounds == 2:
        message[0] = jnp.where(left, lev + run, lev)
        return
    for i, m in enumerate(message_of(lev, run, left, rounds == 1)):
        message[i] = m


def pair_body(total, message, near, out):
    both = log_add(message[0], near[0])
    own = total[...]
    out[0] = both + jnp.where(chip_of() == 1, own, jnp.where(chip_of() == 2, -own, 0.0))


def merge_body(step, rounds, level, total, state, got, state2, message, *group):
    left = (chip_of() >> step) % 2 == 0
    lev, tot, other_lev, other_tot = level[...], total[...], got[0], got[1]
    if state is None:
        zero = jnp.zeros_like(lev)
        before, after, sum_before, sum_after = zero + NEG, zero + NEG, zero, zero
    else:
        before, after, sum_before, sum_after = (state[i] for i in range(4))
    state2[0] = jnp.where(left, before, log_add(before, other_lev + other_tot + sum_before))
    state2[1] = jnp.where(left, log_add(after, other_lev - sum_after), after)
    state2[2] = jnp.where(left, sum_before, sum_before + other_tot)
    state2[3] = jnp.where(left, sum_after + other_tot, sum_after)
    first_lev, first_tot = jnp.where(left, lev, other_lev), jnp.where(left, tot, other_tot)
    second_lev = jnp.where(left, other_lev, lev)
    lev2 = log_add(first_lev, second_lev - first_tot)
    tot2 = tot + other_tot
    for out, value in zip(group, (lev2, tot2)):
        out[...] = value
    next_left = (chip_of() >> (step + 1)) % 2 == 0
    for i, m in enumerate(message_of(lev2, tot2, next_left, step + 2 == rounds)):
        message[i] = m


def joined(rounds, state, got, zero):
    if state is None:
        before, after, sum_before, sum_after = zero + NEG, zero + NEG, zero, zero
    else:
        before, after, sum_before, sum_after = (state[i] for i in range(4))
    if got is not None:
        left = (chip_of() >> (rounds - 1)) % 2 == 0
        other = got[0]
        before = jnp.where(left, before, log_add(before, other + sum_before))
        after = jnp.where(left, log_add(after, other - sum_after), after)
    return before, after, sum_before


def joined_four(near, far, beside, across):
    first, left = chip_of() % 2 == 0, chip_of() < 2
    shift = jnp.where(first == left, beside[...], across[...])
    near, far = near[0], far[0] + jnp.where(left, -shift, shift)
    both, none = log_add(near, far), jnp.zeros_like(near) + NEG
    before = jnp.where(left, jnp.where(first, none, near), jnp.where(first, far, both))
    after = jnp.where(left, jnp.where(first, both, far), jnp.where(first, near, none))
    return before, after, jnp.where(first, 0.0, beside[...])


def tail_body(join, score, level, total, *refs):
    *given, out = refs
    lev, tot = level[...], total[...]
    before, after, sum_before = join(*given, jnp.zeros_like(lev))
    later = after - tot
    norm = log_add(log_add(before, lev), later)
    run = jnp.exp(later - norm)
    half = score.shape[1]
    for i in reversed(range(score.shape[0])):
        run = run + jnp.exp(score[i] - norm)
        out[i * half : (i + 1) * half, :] = run.astype(bf16).astype(f32)
    smoothed = TEMP * (norm - sum_before)
    at = score.shape[0] * half
    out[at : at + STAT_ROWS, :] = jnp.zeros((STAT_ROWS, smoothed.shape[1]), f32)
    out[at : at + 1, :] = jnp.sum(smoothed, axis=0, keepdims=True)
    out[at + 1 : at + 2, :] = jnp.sum(smoothed * smoothed, axis=0, keepdims=True)


def halves_body(chips, features, send):
    width = features.shape[2] // (2 * chips)
    for z in range(chips):
        at = pl.multiple_of((2 * z + 1 - core_of()) * width, width)
        send[:, :, z * width : (z + 1) * width] = features[:, :, pl.ds(at, width)].astype(f32)


def columns_body(chips, features, got, columns):
    dates, paths, whole = features.shape
    half, width = paths // 2, whole // (2 * chips)
    size = dates * half
    for z in range(chips):
        at = pl.multiple_of((2 * z + core_of()) * width, width)
        rows = slice(z * width, (z + 1) * width)
        for h in range(2):
            span = slice(h * half, (h + 1) * half)
            own = features[:, span, pl.ds(at, width)].reshape(size, width).T
            columns[rows, pl.ds(pl.multiple_of((2 * h + core_of()) * size, size), size)] = own
            other = got[:, span, rows].astype(bf16).reshape(size, width).T
            columns[rows, pl.ds(pl.multiple_of((2 * h + 1 - core_of()) * size, size), size)] = other


def side(columns, rows, half):
    size = columns.shape[1] // 2
    return columns[rows, pl.ds(pl.multiple_of(half * size, size), size)]


def first_body(scale, columns, own, out):
    size = columns.shape[1] // 2
    right = own[:size, :].astype(bf16)
    step = columns.shape[0] // FIRST
    for i in range(FIRST):
        rows = slice(i * step, (i + 1) * step)
        out[rows, :] = scale * jnp.dot(side(columns, rows, core_of()), right, preferred_element_type=f32)


def rows_of(scale, j, width, columns, begun, right):
    chip = partner(chip_of(), j, begun.shape[0] // width)
    at = pl.ds(pl.multiple_of(chip * width, width), width)
    return begun[at, :] + scale * jnp.dot(side(columns, at, 1 - core_of()), right, preferred_element_type=f32)


def far_body(scale, far, columns, begun, own, got, keep, message, product):
    size = columns.shape[1] // 2
    right = got[:size, :].astype(bf16)
    _, count, rows, _ = product.shape
    for k, j in enumerate(far):
        product[k] = rows_of(scale, j, count * rows, columns, begun, right).reshape(product.shape[1:])
    halve(0, False, product, own[size:, :] + got[size:, :], keep, message)


def near_body(scale, near, columns, begun, got, *outs):
    right = got[: columns.shape[1] // 2, :].astype(bf16)
    for j, out in zip(near, outs):
        out[...] = rows_of(scale, j, out.shape[0], columns, begun, right)


def path_bits(count, near):
    bits = list(range(count.bit_length() - 1))
    orders = bits, bits[len(bits) // 2 :] + bits[: len(bits) // 2]
    return orders[::-1] if near else orders


def halve(step, near, product, stats, keep, message):
    chips, n, rows, _ = product.shape
    first, second = path_bits(lax.axis_size("path"), near)
    bit, place = (
        jnp.where(core_of() == 0, a, b)
        for a, b in (
            (first[step], second[step]),
            tuple(sum(x < order[step] for x in order[step + 1 :]) for order in (first, second)),
        )
    )
    mine = (lax.axis_index("path") >> bit) & 1
    for out, value in ((keep, mine), (message, 1 - mine)):
        start = 0
        for k in range(chips):
            for i in range(n // 2):
                low = i & ((1 << place) - 1)
                out[start : start + rows, :] = product[k, ((i - low) << 1) + (value << place) + low]
                start += rows
        if stats is not None:
            out[start:, :] = stats


def path_pairs(chips, count, step, near):
    first, second = path_bits(count, near)
    return [
        ((2 * z + core) * count + p, (2 * z + core) * count + (p ^ (1 << order[step])))
        for z in range(chips)
        for core, order in enumerate((first, second))
        for p in range(count)
    ]


def path_sum_body(step, near, *refs):
    *given, keep, message, product = refs
    size = product.shape[0] * product.shape[1] * product.shape[2]
    total = functools.reduce(lambda a, b: a + b, (p[...] for p in given))
    product[...] = total[:size, :].reshape(product.shape)
    halve(step, near, product, total[size:, :] if total.shape[0] > size else None, keep, message)


def partner(me, j, count):
    if count & (count - 1) == 0:
        return me ^ j
    return lax.rem(me + j, count)


def pairs(count, j):
    if count & (count - 1) == 0:
        return [(i, i ^ j) for i in range(count)]
    return [(i, (i + j) % count) for i in range(count)]


def date_pairs(chips, j):
    return [(2 * a + core, 2 * b + core) for a, b in pairs(chips, j) for core in range(2)]


def inner_pairs():
    inner = [(2 * a + c, 6 - 2 * a + c) for a in (1, 2) for c in range(2)]
    return inner + [(2 * a + c, 2 * a + 1 - c) for a in (0, 3) for c in range(2)]


def part_sum_body(rows, mine, got, *outs):
    total = mine[...] + got[...]
    chips = len(outs) - 1
    for k, out in enumerate(outs[:chips]):
        out[0:rows, :] = total[k * rows : (k + 1) * rows, :]
        out[rows:, :] = total[chips * rows :, :]
    outs[-1][...] = total[chips * rows :, :]


def date_sum_body(chips, paths_total, stats, across, *refs):
    parts, (gradient, bound, spread) = refs[:-3], refs[-3:]
    rows = gradient.shape[0]
    gradient[...] = functools.reduce(lambda a, b: a + b, (p[:rows, :] for p in parts), across[:rows, :])
    sums = jnp.where(chip_of() < chips // 2, stats[...], across[rows:, :])
    mean = sums[0:1, :] * (1.0 / paths_total)
    bound[...] = mean
    spread[...] = sums[1:2, :] * (1.0 / paths_total) - mean * mean


def shards(features, payoff, coefficients, exercise):
    dates, paths, width = features.shape
    contracts = coefficients.shape[1]
    chips, count = lax.axis_size("date") // 2, lax.axis_size("path")
    rounds = chips.bit_length() - 1
    assert chips == 1 << rounds
    half, paths_total = paths // 2, paths * count
    rows = width // (2 * chips * count)
    cores = [(2 * z + c, 2 * z + 1 - c) for z in range(chips) for c in range(2)]
    plane = (half, contracts)

    halves = (dates, half, width)
    send, theirs, weights = call(
        theirs_body,
        [((2 * dates, *plane), f32), (halves, bf16), (coefficients.shape, bf16)],
        *(in_hbm(x) for x in (features, coefficients, payoff, exercise)),
        scratch=[
            pltpu.VMEM((dates, half, contracts), f32),
            pltpu.VMEM(exercise.shape, jnp.int32),
            pltpu.SemaphoreType.DMA((2 * PIECES,)),
            pltpu.SemaphoreType.DMA((2,)),
        ],
        place=[pltpu.HBM] * 4,
    )
    other = lax.ppermute(send, "date", cores)
    keep, held = call(
        mine_body,
        [((2 * dates, *plane), f32), (features.shape, bf16)],
        *(in_hbm(x) for x in (features, payoff, exercise)),
        weights,
        theirs,
        scratch=[
            pltpu.VMEM((dates, half, contracts), f32),
            pltpu.VMEM(exercise.shape, jnp.int32),
            pltpu.SemaphoreType.DMA((3,)),
        ],
        place=[pltpu.HBM] * 3,
    )
    sizes = [1 if step + 1 == rounds or rounds == 2 else 2 for step in range(rounds)] or [2]
    score, level, total, message = call(
        functools.partial(local_body, rounds),
        [((2 * dates, *plane), f32), (plane, f32), (plane, f32), ((sizes[0], *plane), f32)],
        keep,
        other,
    )
    (columns_send,) = call(
        functools.partial(halves_body, chips),
        [((dates, paths, width // 2), f32)],
        held,
        message,
        unread=1,
    )
    columns_got = lax.ppermute(columns_send, "date", cores)
    own_level, own_total, state, got = level, total, None, None
    if rounds == 2:
        near = lax.ppermute(message, "date", date_pairs(chips, 1))
        beside = lax.ppermute(total, "date", date_pairs(chips, 1))
        across = lax.ppermute(total, "date", inner_pairs())
        (message,) = call(pair_body, [((1, *plane), f32)], total, message, near)
        far = lax.ppermute(message, "date", date_pairs(chips, 2))
        given, turn = [near, far, beside, across], [beside, across]
        join = lambda *refs: joined_four(*refs[:4])
    else:
        for step in range(rounds):
            got = lax.ppermute(message, "date", date_pairs(chips, 1 << step))
            if step + 1 == rounds:
                break
            body = functools.partial(merge_body, step, rounds)
            if state is None:
                body = lambda a, b, c, *o, body=body: body(a, b, None, c, *o)
            operands = [level, total, got] if state is None else [level, total, state, got]
            group = [(plane, f32)] * (0 if step + 2 == rounds else 2)
            state, message, *group = call(
                body, [((4, *plane), f32), ((sizes[step + 1], *plane), f32)] + group, *operands
            )
            level, total = group or (level, total)
        given, turn = [x for x in (state, got) if x is not None], [message]

        def join(*refs, joined=joined):
            *refs, zero = refs
            held = refs[0] if state is not None else None
            return joined(rounds, held, refs[-1] if got is not None else None, zero)

    (columns,) = call(
        functools.partial(columns_body, chips),
        [((width // 2, 2 * dates * paths), bf16)],
        held,
        columns_got,
        *turn,
        unread=len(turn),
        flops=1 << 27,
    )
    (tail,) = call(
        functools.partial(tail_body, join),
        [((2 * dates * half + STAT_ROWS, contracts), f32)],
        score,
        own_level,
        own_total,
        *given,
        columns,
        unread=1,
    )
    tail_other = lax.ppermute(tail, "date", cores)
    steps = count.bit_length() - 1
    assert count == 1 << steps and steps > 0
    near, far = list(range(chips // 2)), list(range(chips // 2, chips))

    def piece(n, part, stats=False):
        return ((n * part * rows + (STAT_ROWS if stats else 0), contracts), f32)

    def over_path(step, message, near=False):
        return lax.ppermute(message, ("date", "path"), path_pairs(chips, count, step, near))

    def next_round(step, given, after, part, stats):
        n = count >> step
        return call(
            functools.partial(path_sum_body, step, not stats),
            [piece(n // 2, part, stats)] * 2,
            *given,
            *after,
            unread=len(after),
            scratch=[pltpu.VMEM((part, n, rows, contracts), f32)],
        )

    (begun,) = call(
        functools.partial(first_body, -1.0 / paths_total),
        [((width // 2, contracts), f32)],
        columns,
        tail,
        flops=dates * paths * width * contracts,
    )
    keep, message = call(
        functools.partial(far_body, -1.0 / paths_total, far),
        [piece(count // 2, len(far), True)] * 2,
        columns,
        begun,
        tail,
        tail_other,
        scratch=[pltpu.VMEM((len(far), count, rows, contracts), f32)],
        flops=dates * paths * width * contracts // 2,
    )
    got = over_path(0, message)
    firsts = call(
        functools.partial(near_body, -1.0 / paths_total, near),
        [piece(count, 1)] * len(near),
        columns,
        begun,
        tail_other,
        message,
        unread=1,
        flops=dates * paths * width * contracts // 2,
    )
    near_parts = [lax.ppermute(x, "date", date_pairs(chips, j)) if j else x for j, x in zip(near, firsts)]
    assert steps > 1
    for step in range(1, steps):
        keep, message = next_round(step, [keep, got], [], len(far), True)
        got = over_path(step, message)
        near_keep, near_message = next_round(step - 1, near_parts, [message], 1, False)
        near_parts = [near_keep, over_path(step - 1, near_message, True)]
    *sums, stats = call(
        functools.partial(part_sum_body, rows),
        [piece(1, 1, True)] * len(far) + [((STAT_ROWS, contracts), f32)],
        keep,
        got,
        near_message,
        unread=1,
    )
    over = [lax.ppermute(x, "date", date_pairs(chips, j)) for j, x in zip(far, sums)]
    near_keep, near_message = next_round(steps - 1, near_parts, sums[:1], 1, False)
    over += [near_keep, over_path(steps - 1, near_message, True)]
    gradient, bound, spread = call(
        functools.partial(date_sum_body, chips, paths_total),
        [((rows, contracts), f32), ((1, contracts), f32), ((1, contracts), f32)],
        stats,
        *over,
    )
    return gradient, bound.reshape(contracts), spread.reshape(contracts)


def solution(mesh):
    placed = (P("date", "path", None), P("date", "path", None), P(), P("date", None))
    return jax.shard_map(
        shards,
        mesh=mesh,
        in_specs=placed,
        out_specs=(P(("date", "path"), None), P(), P()),
        check_vma=False,
    )
```

```python
import functools

import jax
import jax.numpy as jnp
from jax import lax
from jax.experimental import pallas as pl
from jax.experimental.pallas import tpu as pltpu
from jax.sharding import PartitionSpec as P

INVERSE_TEMP = 4.0
TEMP = 0.25
NEG = -1e30
STAT_ROWS = 8
PIECES = 2
FIRST = 4
VMEM_LIMIT = 16 << 20
f32 = jnp.float32
bf16 = jnp.bfloat16


def core_of():
    return lax.axis_index("date") % 2


def chip_of():
    return lax.axis_index("date") // 2


def in_hbm(x):
    return pltpu.with_memory_space_constraint(x, pltpu.HBM)


def call(body, outs, *operands, scratch=(), flops=0, unread=0, place=()):
    whole = pl.BlockSpec(memory_space=pltpu.VMEM)
    anywhere = pl.BlockSpec(memory_space=pl.ANY)
    read = len(operands) - unread

    def kernel(*refs):
        body(*refs[:read], *refs[read + unread :])

    specs = [pl.BlockSpec(memory_space=p) for p in place]
    return pl.pallas_call(
        kernel,
        out_shape=[jax.ShapeDtypeStruct(*o) for o in outs],
        in_specs=specs + [whole] * (read - len(specs)) + [anywhere] * unread,
        out_specs=[whole] * len(outs),
        scratch_shapes=list(scratch),
        compiler_params=pltpu.CompilerParams(vmem_limit_bytes=VMEM_LIMIT),
        cost_estimate=pl.CostEstimate(flops=flops, bytes_accessed=0, transcendentals=0),
    )(*operands)


def log_add(a, b):
    return jnp.maximum(a, b) + jnp.log(1.0 + jnp.exp(-jnp.abs(a - b)))


def fill(out, inc, pay, may):
    dates = inc.shape[0]
    out[0:dates] = INVERSE_TEMP * inc
    for d in range(dates):
        out[dates + d] = jnp.where(may[d : d + 1, :] > 0, INVERSE_TEMP * pay[d], NEG)


def theirs_body(features, coefficients, payoff, exercise, send, held, weights, pay, may, sems, others):
    dates, paths, width = features.shape
    half, step = paths // 2, width // PIECES
    rows = pl.ds(pl.multiple_of((1 - core_of()) * half, half), half)
    parts = [slice(i * step, (i + 1) * step) for i in range(PIECES)]
    copies = [
        (
            pltpu.make_async_copy(features.at[:, rows, at], held.at[:, :, at], sems.at[2 * i]),
            pltpu.make_async_copy(coefficients.at[at, :], weights.at[at, :], sems.at[2 * i + 1]),
        )
        for i, at in enumerate(parts)
    ]
    small = (
        pltpu.make_async_copy(payoff.at[:, rows, :], pay, others.at[0]),
        pltpu.make_async_copy(exercise, may, others.at[1]),
    )
    for c in (*(c for pair in copies for c in pair), *small):
        c.start()
    inc = None
    for pair, at in zip(copies, parts):
        for c in pair:
            c.wait()
        left = held[:, :, at].reshape(dates * half, step)
        part = jnp.dot(left, weights[at, :], preferred_element_type=f32)
        inc = part if inc is None else inc + part
    for c in small:
        c.wait()
    fill(send, inc.reshape(dates, half, -1), pay, may)


def mine_body(features, payoff, exercise, weights, theirs, keep, held, pay, may, sems):
    dates, paths, width = features.shape
    half = paths // 2
    rows = pl.ds(pl.multiple_of(core_of() * half, half), half)
    copies = (
        pltpu.make_async_copy(features.at[:, rows, :], held.at[:, rows, :], sems.at[0]),
        pltpu.make_async_copy(payoff.at[:, rows, :], pay, sems.at[1]),
        pltpu.make_async_copy(exercise, may, sems.at[2]),
    )
    for c in copies:
        c.start()
    held[:, pl.ds(pl.multiple_of((1 - core_of()) * half, half), half), :] = theirs[...]
    for c in copies:
        c.wait()
    inc = jnp.dot(held[:, rows, :].reshape(dates * half, width), weights[...], preferred_element_type=f32)
    fill(keep, inc.reshape(dates, half, -1), pay, may)


def message_of(level, total, left, last):
    if last:
        return [jnp.where(left, level + total, level)]
    return [level, total]


def local_body(rounds, keep, other, since, peak_out, level, total, message):
    dates = keep.shape[0] // 2
    first = core_of() == 0
    run = jnp.zeros(keep.shape[1:], f32)
    scores = []
    for part in (0, 1):
        for d in range(dates):
            inc, base = (
                jnp.where(first == (part == 0), keep[at], other[at]) for at in (d, dates + d)
            )
            run = run + inc
            scores.append(base - run)
    peak = functools.reduce(jnp.maximum, scores)
    run_since = jnp.zeros_like(peak)
    for i in reversed(range(len(scores))):
        run_since = run_since + jnp.exp(scores[i] - peak)
        since[i] = run_since
    lev = peak + jnp.log(run_since)
    peak_out[...] = peak
    level[...] = lev
    total[...] = run
    left = chip_of() % 2 == 0
    if rounds == 2:
        message[0] = jnp.where(left, lev + run, lev)
        return
    for i, m in enumerate(message_of(lev, run, left, rounds == 1)):
        message[i] = m


def pair_body(total, message, near, out):
    both = log_add(message[0], near[0])
    own = total[...]
    out[0] = both + jnp.where(chip_of() == 1, own, jnp.where(chip_of() == 2, -own, 0.0))


def merge_body(step, rounds, level, total, state, got, state2, message, *group):
    left = (chip_of() >> step) % 2 == 0
    lev, tot, other_lev, other_tot = level[...], total[...], got[0], got[1]
    if state is None:
        zero = jnp.zeros_like(lev)
        before, after, sum_before, sum_after = zero + NEG, zero + NEG, zero, zero
    else:
        before, after, sum_before, sum_after = (state[i] for i in range(4))
    state2[0] = jnp.where(left, before, log_add(before, other_lev + other_tot + sum_before))
    state2[1] = jnp.where(left, log_add(after, other_lev - sum_after), after)
    state2[2] = jnp.where(left, sum_before, sum_before + other_tot)
    state2[3] = jnp.where(left, sum_after + other_tot, sum_after)
    first_lev, first_tot = jnp.where(left, lev, other_lev), jnp.where(left, tot, other_tot)
    second_lev = jnp.where(left, other_lev, lev)
    lev2 = log_add(first_lev, second_lev - first_tot)
    tot2 = tot + other_tot
    for out, value in zip(group, (lev2, tot2)):
        out[...] = value
    next_left = (chip_of() >> (step + 1)) % 2 == 0
    for i, m in enumerate(message_of(lev2, tot2, next_left, step + 2 == rounds)):
        message[i] = m


def joined(rounds, state, got, zero):
    if state is None:
        before, after, sum_before, sum_after = zero + NEG, zero + NEG, zero, zero
    else:
        before, after, sum_before, sum_after = (state[i] for i in range(4))
    if got is not None:
        left = (chip_of() >> (rounds - 1)) % 2 == 0
        other = got[0]
        before = jnp.where(left, before, log_add(before, other + sum_before))
        after = jnp.where(left, log_add(after, other - sum_after), after)
    return before, after, sum_before


def joined_four(near, far, beside, across):
    first, left = chip_of() % 2 == 0, chip_of() < 2
    shift = jnp.where(first == left, beside[...], across[...])
    near, far = near[0], far[0] + jnp.where(left, -shift, shift)
    both, none = log_add(near, far), jnp.zeros_like(near) + NEG
    before = jnp.where(left, jnp.where(first, none, near), jnp.where(first, far, both))
    after = jnp.where(left, jnp.where(first, both, far), jnp.where(first, near, none))
    return before, after, jnp.where(first, 0.0, beside[...])


def tail_body(join, since, peak, level, total, *refs):
    *given, out = refs
    lev, tot = level[...], total[...]
    before, after, sum_before = join(*given, jnp.zeros_like(lev))
    later = after - tot
    norm = log_add(log_add(before, lev), later)
    rest, factor = jnp.exp(later - norm), jnp.exp(peak[...] - norm)
    half = since.shape[1]
    for i in range(since.shape[0]):
        run = rest + factor * since[i]
        out[i * half : (i + 1) * half, :] = run.astype(bf16).astype(f32)
    smoothed = TEMP * (norm - sum_before)
    at = since.shape[0] * half
    out[at : at + STAT_ROWS, :] = jnp.zeros((STAT_ROWS, smoothed.shape[1]), f32)
    out[at : at + 1, :] = jnp.sum(smoothed, axis=0, keepdims=True)
    out[at + 1 : at + 2, :] = jnp.sum(smoothed * smoothed, axis=0, keepdims=True)


def halves_body(chips, features, send):
    width = features.shape[2] // (2 * chips)
    for z in range(chips):
        at = pl.multiple_of((2 * z + 1 - core_of()) * width, width)
        send[:, :, z * width : (z + 1) * width] = features[:, :, pl.ds(at, width)].astype(f32)


def columns_body(chips, features, got, columns):
    dates, paths, whole = features.shape
    half, width = paths // 2, whole // (2 * chips)
    size = dates * half
    for z in range(chips):
        at = pl.multiple_of((2 * z + core_of()) * width, width)
        rows = slice(z * width, (z + 1) * width)
        for h in range(2):
            span = slice(h * half, (h + 1) * half)
            own = features[:, span, pl.ds(at, width)].reshape(size, width).T
            columns[rows, pl.ds(pl.multiple_of((2 * h + core_of()) * size, size), size)] = own
            other = got[:, span, rows].astype(bf16).reshape(size, width).T
            columns[rows, pl.ds(pl.multiple_of((2 * h + 1 - core_of()) * size, size), size)] = other


def side(columns, rows, half):
    size = columns.shape[1] // 2
    return columns[rows, pl.ds(pl.multiple_of(half * size, size), size)]


def first_body(scale, columns, own, out):
    size = columns.shape[1] // 2
    right = own[:size, :].astype(bf16)
    step = columns.shape[0] // FIRST
    for i in range(FIRST):
        rows = slice(i * step, (i + 1) * step)
        out[rows, :] = scale * jnp.dot(side(columns, rows, core_of()), right, preferred_element_type=f32)


def rows_of(scale, j, width, columns, begun, right):
    chip = partner(chip_of(), j, begun.shape[0] // width)
    at = pl.ds(pl.multiple_of(chip * width, width), width)
    return begun[at, :] + scale * jnp.dot(side(columns, at, 1 - core_of()), right, preferred_element_type=f32)


def far_body(scale, far, columns, begun, own, got, keep, message, product):
    size = columns.shape[1] // 2
    right = got[:size, :].astype(bf16)
    _, count, rows, _ = product.shape
    for k, j in enumerate(far):
        product[k] = rows_of(scale, j, count * rows, columns, begun, right).reshape(product.shape[1:])
    halve(0, False, product, own[size:, :] + got[size:, :], keep, message)


def near_body(scale, near, columns, begun, got, *outs):
    right = got[: columns.shape[1] // 2, :].astype(bf16)
    for j, out in zip(near, outs):
        out[...] = rows_of(scale, j, out.shape[0], columns, begun, right)


def path_bits(count, near):
    bits = list(range(count.bit_length() - 1))
    orders = bits, bits[len(bits) // 2 :] + bits[: len(bits) // 2]
    return orders[::-1] if near else orders


def halve(step, near, product, stats, keep, message):
    chips, n, rows, _ = product.shape
    first, second = path_bits(lax.axis_size("path"), near)
    bit, place = (
        jnp.where(core_of() == 0, a, b)
        for a, b in (
            (first[step], second[step]),
            tuple(sum(x < order[step] for x in order[step + 1 :]) for order in (first, second)),
        )
    )
    mine = (lax.axis_index("path") >> bit) & 1
    for out, value in ((keep, mine), (message, 1 - mine)):
        start = 0
        for k in range(chips):
            for i in range(n // 2):
                low = i & ((1 << place) - 1)
                out[start : start + rows, :] = product[k, ((i - low) << 1) + (value << place) + low]
                start += rows
        if stats is not None:
            out[start:, :] = stats


def path_pairs(chips, count, step, near):
    first, second = path_bits(count, near)
    return [
        ((2 * z + core) * count + p, (2 * z + core) * count + (p ^ (1 << order[step])))
        for z in range(chips)
        for core, order in enumerate((first, second))
        for p in range(count)
    ]


def path_sum_body(step, near, *refs):
    *given, keep, message, product = refs
    size = product.shape[0] * product.shape[1] * product.shape[2]
    total = functools.reduce(lambda a, b: a + b, (p[...] for p in given))
    product[...] = total[:size, :].reshape(product.shape)
    halve(step, near, product, total[size:, :] if total.shape[0] > size else None, keep, message)


def partner(me, j, count):
    if count & (count - 1) == 0:
        return me ^ j
    return lax.rem(me + j, count)


def pairs(count, j):
    if count & (count - 1) == 0:
        return [(i, i ^ j) for i in range(count)]
    return [(i, (i + j) % count) for i in range(count)]


def date_pairs(chips, j):
    return [(2 * a + core, 2 * b + core) for a, b in pairs(chips, j) for core in range(2)]


def inner_pairs():
    inner = [(2 * a + c, 6 - 2 * a + c) for a in (1, 2) for c in range(2)]
    return inner + [(2 * a + c, 2 * a + 1 - c) for a in (0, 3) for c in range(2)]


def part_sum_body(rows, mine, got, *outs):
    total = mine[...] + got[...]
    *messages, stats = outs
    half = total.shape[1] // 2
    sums = total[len(messages) * rows :, :]
    for k, out in enumerate(messages):
        block = total[k * rows : (k + 1) * rows, :]
        out[2 * rows :, :] = jnp.zeros((STAT_ROWS, half), f32)
        for side_, columns in enumerate((slice(0, half), slice(half, None))):
            out[side_ * rows : (side_ + 1) * rows, :] = block[:, columns]
            out[2 * rows + 2 * side_ : 2 * rows + 2 * side_ + 2, :] = sums[0:2, columns]
    stats[...] = sums


def date_sum_body(chips, far, paths_total, stats, *refs):
    parts, (gradient, bound, spread) = refs[:-3], refs[-3:]
    rows, contracts = gradient.shape
    half = contracts // 2
    first = chip_of() < chips // 2
    for side_, columns in enumerate((slice(0, half), slice(half, contracts))):
        at, behind = side_ * rows, 2 * rows + 2 * side_
        total = functools.reduce(lambda a, b: a + b, (p[:, columns] for p in parts[far:]))
        gradient[:, columns] = functools.reduce(lambda a, b: a + b, (p[at : at + rows, :] for p in parts[:far]), total)
        sums = jnp.where(first, stats[0:2, columns], parts[0][behind : behind + 2, :])
        mean = sums[0:1, :] * (1.0 / paths_total)
        bound[:, columns] = mean
        spread[:, columns] = sums[1:2, :] * (1.0 / paths_total) - mean * mean


def shards(features, payoff, coefficients, exercise):
    dates, paths, width = features.shape
    contracts = coefficients.shape[1]
    chips, count = lax.axis_size("date") // 2, lax.axis_size("path")
    rounds = chips.bit_length() - 1
    assert chips == 1 << rounds
    half, paths_total = paths // 2, paths * count
    rows = width // (2 * chips * count)
    cores = [(2 * z + c, 2 * z + 1 - c) for z in range(chips) for c in range(2)]
    plane = (half, contracts)

    halves = (dates, half, width)
    send, theirs, weights = call(
        theirs_body,
        [((2 * dates, *plane), f32), (halves, bf16), (coefficients.shape, bf16)],
        *(in_hbm(x) for x in (features, coefficients, payoff, exercise)),
        scratch=[
            pltpu.VMEM((dates, half, contracts), f32),
            pltpu.VMEM(exercise.shape, jnp.int32),
            pltpu.SemaphoreType.DMA((2 * PIECES,)),
            pltpu.SemaphoreType.DMA((2,)),
        ],
        place=[pltpu.HBM] * 4,
    )
    other = lax.ppermute(send, "date", cores)
    keep, held = call(
        mine_body,
        [((2 * dates, *plane), f32), (features.shape, bf16)],
        *(in_hbm(x) for x in (features, payoff, exercise)),
        weights,
        theirs,
        scratch=[
            pltpu.VMEM((dates, half, contracts), f32),
            pltpu.VMEM(exercise.shape, jnp.int32),
            pltpu.SemaphoreType.DMA((3,)),
        ],
        place=[pltpu.HBM] * 3,
    )
    sizes = [1 if step + 1 == rounds or rounds == 2 else 2 for step in range(rounds)] or [2]
    since, peak, level, total, message = call(
        functools.partial(local_body, rounds),
        [((2 * dates, *plane), f32)] + [(plane, f32)] * 3 + [((sizes[0], *plane), f32)],
        keep,
        other,
    )
    (columns_send,) = call(
        functools.partial(halves_body, chips),
        [((dates, paths, width // 2), f32)],
        held,
        message,
        unread=1,
    )
    columns_got = lax.ppermute(columns_send, "date", cores)
    own_level, own_total, state, got = level, total, None, None
    if rounds == 2:
        near = lax.ppermute(message, "date", date_pairs(chips, 1))
        beside = lax.ppermute(total, "date", date_pairs(chips, 1))
        across = lax.ppermute(total, "date", inner_pairs())
        (message,) = call(pair_body, [((1, *plane), f32)], total, message, near)
        far = lax.ppermute(message, "date", date_pairs(chips, 2))
        given, turn = [near, far, beside, across], [beside, across]
        join = lambda *refs: joined_four(*refs[:4])
    else:
        for step in range(rounds):
            got = lax.ppermute(message, "date", date_pairs(chips, 1 << step))
            if step + 1 == rounds:
                break
            body = functools.partial(merge_body, step, rounds)
            if state is None:
                body = lambda a, b, c, *o, body=body: body(a, b, None, c, *o)
            operands = [level, total, got] if state is None else [level, total, state, got]
            group = [(plane, f32)] * (0 if step + 2 == rounds else 2)
            state, message, *group = call(
                body, [((4, *plane), f32), ((sizes[step + 1], *plane), f32)] + group, *operands
            )
            level, total = group or (level, total)
        given, turn = [x for x in (state, got) if x is not None], [message]

        def join(*refs, joined=joined):
            *refs, zero = refs
            held = refs[0] if state is not None else None
            return joined(rounds, held, refs[-1] if got is not None else None, zero)

    (columns,) = call(
        functools.partial(columns_body, chips),
        [((width // 2, 2 * dates * paths), bf16)],
        held,
        columns_got,
        *turn,
        unread=len(turn),
        flops=1 << 27,
    )
    (tail,) = call(
        functools.partial(tail_body, join),
        [((2 * dates * half + STAT_ROWS, contracts), f32)],
        since,
        peak,
        own_level,
        own_total,
        *given,
        columns,
        unread=1,
    )
    tail_other = lax.ppermute(tail, "date", cores)
    steps = count.bit_length() - 1
    assert count == 1 << steps and steps > 0
    near, far = list(range(chips // 2)), list(range(chips // 2, chips))

    def piece(n, part, stats=False):
        return ((n * part * rows + (STAT_ROWS if stats else 0), contracts), f32)

    def over_path(step, message, near=False):
        return lax.ppermute(message, ("date", "path"), path_pairs(chips, count, step, near))

    def next_round(step, given, after, part, stats):
        n = count >> step
        return call(
            functools.partial(path_sum_body, step, not stats),
            [piece(n // 2, part, stats)] * 2,
            *given,
            *after,
            unread=len(after),
            scratch=[pltpu.VMEM((part, n, rows, contracts), f32)],
        )

    (begun,) = call(
        functools.partial(first_body, -1.0 / paths_total),
        [((width // 2, contracts), f32)],
        columns,
        tail,
        flops=dates * paths * width * contracts,
    )
    keep, message = call(
        functools.partial(far_body, -1.0 / paths_total, far),
        [piece(count // 2, len(far), True)] * 2,
        columns,
        begun,
        tail,
        tail_other,
        scratch=[pltpu.VMEM((len(far), count, rows, contracts), f32)],
        flops=dates * paths * width * contracts // 2,
    )
    got = over_path(0, message)
    firsts = call(
        functools.partial(near_body, -1.0 / paths_total, near),
        [piece(count, 1)] * len(near),
        columns,
        begun,
        tail_other,
        message,
        unread=1,
        flops=dates * paths * width * contracts // 2,
    )
    near_parts = [lax.ppermute(x, "date", date_pairs(chips, j)) if j else x for j, x in zip(near, firsts)]
    assert steps > 1
    for step in range(1, steps):
        keep, message = next_round(step, [keep, got], [], len(far), True)
        got = over_path(step, message)
        near_keep, near_message = next_round(step - 1, near_parts, [message], 1, False)
        near_parts = [near_keep, over_path(step - 1, near_message, True)]
    *sums, stats = call(
        functools.partial(part_sum_body, rows),
        [((2 * rows + STAT_ROWS, contracts // 2), f32)] * len(far) + [((STAT_ROWS, contracts), f32)],
        keep,
        got,
        near_message,
        unread=1,
    )
    over = [lax.ppermute(x, "date", date_pairs(chips, j)) for j, x in zip(far, sums)]
    near_keep, near_message = next_round(steps - 1, near_parts, sums[:1], 1, False)
    over += [near_keep, over_path(steps - 1, near_message, True)]
    gradient, bound, spread = call(
        functools.partial(date_sum_body, chips, len(far), paths_total),
        [((rows, contracts), f32), ((1, contracts), f32), ((1, contracts), f32)],
        stats,
        *over,
    )
    return gradient, bound.reshape(contracts), spread.reshape(contracts)


def solution(mesh):
    placed = (P("date", "path", None), P("date", "path", None), P(), P("date", None))
    return jax.shard_map(
        shards,
        mesh=mesh,
        in_specs=placed,
        out_specs=(P(("date", "path"), None), P(), P()),
        check_vma=False,
    )
```

```python
import functools

import jax
import jax.numpy as jnp
from jax import lax
from jax.experimental import pallas as pl
from jax.experimental.pallas import tpu as pltpu
from jax.sharding import PartitionSpec as P

INVERSE_TEMP = 4.0
TEMP = 0.25
NEG = -1e30
STAT_ROWS = 8
PIECES = 2
FIRST = 4
VMEM_LIMIT = 16 << 20
f32 = jnp.float32
bf16 = jnp.bfloat16


def core_of():
    return lax.axis_index("date") % 2


def chip_of():
    return lax.axis_index("date") // 2


def in_hbm(x):
    return pltpu.with_memory_space_constraint(x, pltpu.HBM)


def call(body, outs, *operands, scratch=(), flops=0, unread=0, place=()):
    whole = pl.BlockSpec(memory_space=pltpu.VMEM)
    anywhere = pl.BlockSpec(memory_space=pl.ANY)
    read = len(operands) - unread

    def kernel(*refs):
        body(*refs[:read], *refs[read + unread :])

    specs = [pl.BlockSpec(memory_space=p) for p in place]
    return pl.pallas_call(
        kernel,
        out_shape=[jax.ShapeDtypeStruct(*o) for o in outs],
        in_specs=specs + [whole] * (read - len(specs)) + [anywhere] * unread,
        out_specs=[whole] * len(outs),
        scratch_shapes=list(scratch),
        compiler_params=pltpu.CompilerParams(vmem_limit_bytes=VMEM_LIMIT),
        cost_estimate=pl.CostEstimate(flops=flops, bytes_accessed=0, transcendentals=0),
    )(*operands)


def log_add(a, b):
    return jnp.maximum(a, b) + jnp.log(1.0 + jnp.exp(-jnp.abs(a - b)))


def fill(out, inc, pay, may):
    dates = inc.shape[0]
    out[0:dates] = INVERSE_TEMP * inc
    for d in range(dates):
        out[dates + d] = jnp.where(may[d : d + 1, :] > 0, INVERSE_TEMP * pay[d], NEG)


def theirs_body(features, coefficients, payoff, exercise, send, held, weights, pay, may, sems, others):
    dates, paths, width = features.shape
    half, step = paths // 2, width // PIECES
    rows = pl.ds(pl.multiple_of((1 - core_of()) * half, half), half)
    parts = [slice(i * step, (i + 1) * step) for i in range(PIECES)]
    copies = [
        (
            pltpu.make_async_copy(features.at[:, rows, at], held.at[:, :, at], sems.at[2 * i]),
            pltpu.make_async_copy(coefficients.at[at, :], weights.at[at, :], sems.at[2 * i + 1]),
        )
        for i, at in enumerate(parts)
    ]
    small = (
        pltpu.make_async_copy(payoff.at[:, rows, :], pay, others.at[0]),
        pltpu.make_async_copy(exercise, may, others.at[1]),
    )
    for c in (*(c for pair in copies for c in pair), *small):
        c.start()
    inc = None
    for pair, at in zip(copies, parts):
        for c in pair:
            c.wait()
        left = held[:, :, at].reshape(dates * half, step)
        part = jnp.dot(left, weights[at, :], preferred_element_type=f32)
        inc = part if inc is None else inc + part
    for c in small:
        c.wait()
    fill(send, inc.reshape(dates, half, -1), pay, may)


def mine_body(features, payoff, exercise, weights, theirs, keep, held, pay, may, sems):
    dates, paths, width = features.shape
    half = paths // 2
    rows = pl.ds(pl.multiple_of(core_of() * half, half), half)
    copies = (
        pltpu.make_async_copy(features.at[:, rows, :], held.at[:, rows, :], sems.at[0]),
        pltpu.make_async_copy(payoff.at[:, rows, :], pay, sems.at[1]),
        pltpu.make_async_copy(exercise, may, sems.at[2]),
    )
    for c in copies:
        c.start()
    held[:, pl.ds(pl.multiple_of((1 - core_of()) * half, half), half), :] = theirs[...]
    for c in copies:
        c.wait()
    inc = jnp.dot(held[:, rows, :].reshape(dates * half, width), weights[...], preferred_element_type=f32)
    fill(keep, inc.reshape(dates, half, -1), pay, may)


def message_of(level, total, left, last):
    if last:
        return [jnp.where(left, level + total, level)]
    return [level, total]


def local_body(rounds, keep, other, since, peak_out, level, total, message):
    dates = keep.shape[0] // 2
    first = core_of() == 0
    run = jnp.zeros(keep.shape[1:], f32)
    scores = []
    for part in (0, 1):
        for d in range(dates):
            inc, base = (
                jnp.where(first == (part == 0), keep[at], other[at]) for at in (d, dates + d)
            )
            run = run + inc
            scores.append(base - run)
    peak = functools.reduce(jnp.maximum, scores)
    run_since = jnp.zeros_like(peak)
    for i in reversed(range(len(scores))):
        run_since = run_since + jnp.exp(scores[i] - peak)
        since[i] = run_since
    lev = peak + jnp.log(run_since)
    peak_out[...] = peak
    level[...] = lev
    total[...] = run
    left = chip_of() % 2 == 0
    if rounds == 2:
        message[0] = jnp.where(left, lev + run, lev)
        return
    for i, m in enumerate(message_of(lev, run, left, rounds == 1)):
        message[i] = m


def pair_body(total, message, near, out):
    both = log_add(message[0], near[0])
    own = total[...]
    out[0] = both + jnp.where(chip_of() == 1, own, jnp.where(chip_of() == 2, -own, 0.0))


def merge_body(step, rounds, level, total, state, got, state2, message, *group):
    left = (chip_of() >> step) % 2 == 0
    lev, tot, other_lev, other_tot = level[...], total[...], got[0], got[1]
    if state is None:
        zero = jnp.zeros_like(lev)
        before, after, sum_before, sum_after = zero + NEG, zero + NEG, zero, zero
    else:
        before, after, sum_before, sum_after = (state[i] for i in range(4))
    state2[0] = jnp.where(left, before, log_add(before, other_lev + other_tot + sum_before))
    state2[1] = jnp.where(left, log_add(after, other_lev - sum_after), after)
    state2[2] = jnp.where(left, sum_before, sum_before + other_tot)
    state2[3] = jnp.where(left, sum_after + other_tot, sum_after)
    first_lev, first_tot = jnp.where(left, lev, other_lev), jnp.where(left, tot, other_tot)
    second_lev = jnp.where(left, other_lev, lev)
    lev2 = log_add(first_lev, second_lev - first_tot)
    tot2 = tot + other_tot
    for out, value in zip(group, (lev2, tot2)):
        out[...] = value
    next_left = (chip_of() >> (step + 1)) % 2 == 0
    for i, m in enumerate(message_of(lev2, tot2, next_left, step + 2 == rounds)):
        message[i] = m


def joined(rounds, state, got, zero):
    if state is None:
        before, after, sum_before, sum_after = zero + NEG, zero + NEG, zero, zero
    else:
        before, after, sum_before, sum_after = (state[i] for i in range(4))
    if got is not None:
        left = (chip_of() >> (rounds - 1)) % 2 == 0
        other = got[0]
        before = jnp.where(left, before, log_add(before, other + sum_before))
        after = jnp.where(left, log_add(after, other - sum_after), after)
    return before, after, sum_before


def joined_four(near, far, beside, across):
    first, left = chip_of() % 2 == 0, chip_of() < 2
    shift = jnp.where(first == left, beside[...], across[...])
    near, far = near[0], far[0] + jnp.where(left, -shift, shift)
    both, none = log_add(near, far), jnp.zeros_like(near) + NEG
    before = jnp.where(left, jnp.where(first, none, near), jnp.where(first, far, both))
    after = jnp.where(left, jnp.where(first, both, far), jnp.where(first, near, none))
    return before, after, jnp.where(first, 0.0, beside[...])


def tail_body(join, since, peak, level, total, *refs):
    *given, out = refs
    lev, tot = level[...], total[...]
    before, after, sum_before = join(*given, jnp.zeros_like(lev))
    later = after - tot
    norm = log_add(log_add(before, lev), later)
    rest, factor = jnp.exp(later - norm), jnp.exp(peak[...] - norm)
    half = since.shape[1]
    for i in range(since.shape[0]):
        run = rest + factor * since[i]
        out[i * half : (i + 1) * half, :] = run.astype(bf16).astype(f32)
    smoothed = TEMP * (norm - sum_before)
    at = since.shape[0] * half
    out[at : at + STAT_ROWS, :] = jnp.zeros((STAT_ROWS, smoothed.shape[1]), f32)
    out[at : at + 1, :] = jnp.sum(smoothed, axis=0, keepdims=True)
    out[at + 1 : at + 2, :] = jnp.sum(smoothed * smoothed, axis=0, keepdims=True)


def halves_body(chips, features, send):
    width = features.shape[2] // (2 * chips)
    for z in range(chips):
        at = pl.multiple_of((2 * z + 1 - core_of()) * width, width)
        send[:, :, z * width : (z + 1) * width] = features[:, :, pl.ds(at, width)].astype(f32)


def columns_body(chips, features, got, columns):
    dates, paths, whole = features.shape
    half, width = paths // 2, whole // (2 * chips)
    size = dates * half
    for z in range(chips):
        at = pl.multiple_of((2 * z + core_of()) * width, width)
        rows = slice(z * width, (z + 1) * width)
        for h in range(2):
            span = slice(h * half, (h + 1) * half)
            own = features[:, span, pl.ds(at, width)].reshape(size, width).T
            columns[rows, pl.ds(pl.multiple_of((2 * h + core_of()) * size, size), size)] = own
            other = got[:, span, rows].astype(bf16).reshape(size, width).T
            columns[rows, pl.ds(pl.multiple_of((2 * h + 1 - core_of()) * size, size), size)] = other


def side(columns, rows, half):
    size = columns.shape[1] // 2
    return columns[rows, pl.ds(pl.multiple_of(half * size, size), size)]


def first_body(scale, columns, own, out):
    size = columns.shape[1] // 2
    right = own[:size, :].astype(bf16)
    step = columns.shape[0] // FIRST
    for i in range(FIRST):
        rows = slice(i * step, (i + 1) * step)
        out[rows, :] = scale * jnp.dot(side(columns, rows, core_of()), right, preferred_element_type=f32)


def rows_of(scale, j, width, columns, begun, right):
    chip = partner(chip_of(), j, begun.shape[0] // width)
    at = pl.ds(pl.multiple_of(chip * width, width), width)
    return begun[at, :] + scale * jnp.dot(side(columns, at, 1 - core_of()), right, preferred_element_type=f32)


def far_half(scale, far, mine, columns, begun, own, got, out, product):
    size = columns.shape[1] // 2
    right = got[:size, :].astype(bf16)
    count, rows, _ = product.shape
    bit, place = round_of(0, False)
    value = (lax.axis_index("path") >> bit) & 1
    value = value if mine else 1 - value
    start = 0
    for j in far:
        chip = partner(chip_of(), j, begun.shape[0] // (count * rows))
        if rows % 16:
            product[...] = rows_of(scale, j, count * rows, columns, begun, right).reshape(product.shape)
        for i in range(count // 2):
            path = place_of(i, value, place)
            if rows % 16:
                block = product[path]
            else:
                at = pl.ds(pl.multiple_of((chip * count + path) * rows, rows), rows)
                block = jnp.dot(side(columns, at, 1 - core_of()), right, preferred_element_type=f32)
                block = begun[at, :] + scale * block
            out[start : start + rows, :] = block
            start += rows
    out[start:, :] = own[size:, :] + got[size:, :]


def near_body(scale, far, near, columns, begun, own, got, keep, *refs):
    *outs, product = refs
    right = got[: columns.shape[1] // 2, :].astype(bf16)
    for j, out in zip(near, outs):
        out[...] = rows_of(scale, j, out.shape[0], columns, begun, right)
    far_half(scale, far, True, columns, begun, own, got, keep, product)


def round_of(step, near):
    first, second = path_bits(lax.axis_size("path"), near)
    return tuple(
        jnp.where(core_of() == 0, a, b)
        for a, b in (
            (first[step], second[step]),
            tuple(sum(x < order[step] for x in order[step + 1 :]) for order in (first, second)),
        )
    )


def place_of(i, value, place):
    low = i & ((1 << place) - 1)
    return ((i - low) << 1) + (value << place) + low


def path_bits(count, near):
    bits = list(range(count.bit_length() - 1))
    orders = bits, bits[len(bits) // 2 :] + bits[: len(bits) // 2]
    return orders[::-1] if near else orders


def halve(step, near, product, stats, keep, message):
    chips, n, rows, _ = product.shape
    bit, place = round_of(step, near)
    mine = (lax.axis_index("path") >> bit) & 1
    for out, value in ((keep, mine), (message, 1 - mine)):
        start = 0
        for k in range(chips):
            for i in range(n // 2):
                out[start : start + rows, :] = product[k, place_of(i, value, place)]
                start += rows
        if stats is not None:
            out[start:, :] = stats


def path_pairs(chips, count, step, near):
    first, second = path_bits(count, near)
    return [
        ((2 * z + core) * count + p, (2 * z + core) * count + (p ^ (1 << order[step])))
        for z in range(chips)
        for core, order in enumerate((first, second))
        for p in range(count)
    ]


def path_sum_body(step, near, *refs):
    *given, keep, message, product = refs
    size = product.shape[0] * product.shape[1] * product.shape[2]
    total = functools.reduce(lambda a, b: a + b, (p[...] for p in given))
    product[...] = total[:size, :].reshape(product.shape)
    halve(step, near, product, total[size:, :] if total.shape[0] > size else None, keep, message)


def partner(me, j, count):
    if count & (count - 1) == 0:
        return me ^ j
    return lax.rem(me + j, count)


def pairs(count, j):
    if count & (count - 1) == 0:
        return [(i, i ^ j) for i in range(count)]
    return [(i, (i + j) % count) for i in range(count)]


def date_pairs(chips, j):
    return [(2 * a + core, 2 * b + core) for a, b in pairs(chips, j) for core in range(2)]


def inner_pairs():
    inner = [(2 * a + c, 6 - 2 * a + c) for a in (1, 2) for c in range(2)]
    return inner + [(2 * a + c, 2 * a + 1 - c) for a in (0, 3) for c in range(2)]


def part_sum_body(rows, mine, got, *outs):
    total = mine[...] + got[...]
    *messages, stats = outs
    half = total.shape[1] // 2
    sums = total[len(messages) * rows :, :]
    for k, out in enumerate(messages):
        block = total[k * rows : (k + 1) * rows, :]
        out[2 * rows :, :] = jnp.zeros((STAT_ROWS, half), f32)
        for side_, columns in enumerate((slice(0, half), slice(half, None))):
            out[side_ * rows : (side_ + 1) * rows, :] = block[:, columns]
            out[2 * rows + 2 * side_ : 2 * rows + 2 * side_ + 2, :] = sums[0:2, columns]
    stats[...] = sums


def date_sum_body(chips, far, paths_total, stats, *refs):
    parts, (gradient, bound, spread) = refs[:-3], refs[-3:]
    rows, contracts = gradient.shape
    half = contracts // 2
    first = chip_of() < chips // 2
    for side_, columns in enumerate((slice(0, half), slice(half, contracts))):
        at, behind = side_ * rows, 2 * rows + 2 * side_
        total = functools.reduce(lambda a, b: a + b, (p[:, columns] for p in parts[far:]))
        gradient[:, columns] = functools.reduce(lambda a, b: a + b, (p[at : at + rows, :] for p in parts[:far]), total)
        sums = jnp.where(first, stats[0:2, columns], parts[0][behind : behind + 2, :])
        mean = sums[0:1, :] * (1.0 / paths_total)
        bound[:, columns] = mean
        spread[:, columns] = sums[1:2, :] * (1.0 / paths_total) - mean * mean


def shards(features, payoff, coefficients, exercise):
    dates, paths, width = features.shape
    contracts = coefficients.shape[1]
    chips, count = lax.axis_size("date") // 2, lax.axis_size("path")
    rounds = chips.bit_length() - 1
    assert chips == 1 << rounds
    half, paths_total = paths // 2, paths * count
    rows = width // (2 * chips * count)
    cores = [(2 * z + c, 2 * z + 1 - c) for z in range(chips) for c in range(2)]
    plane = (half, contracts)

    halves = (dates, half, width)
    send, theirs, weights = call(
        theirs_body,
        [((2 * dates, *plane), f32), (halves, bf16), (coefficients.shape, bf16)],
        *(in_hbm(x) for x in (features, coefficients, payoff, exercise)),
        scratch=[
            pltpu.VMEM((dates, half, contracts), f32),
            pltpu.VMEM(exercise.shape, jnp.int32),
            pltpu.SemaphoreType.DMA((2 * PIECES,)),
            pltpu.SemaphoreType.DMA((2,)),
        ],
        place=[pltpu.HBM] * 4,
    )
    other = lax.ppermute(send, "date", cores)
    keep, held = call(
        mine_body,
        [((2 * dates, *plane), f32), (features.shape, bf16)],
        *(in_hbm(x) for x in (features, payoff, exercise)),
        weights,
        theirs,
        scratch=[
            pltpu.VMEM((dates, half, contracts), f32),
            pltpu.VMEM(exercise.shape, jnp.int32),
            pltpu.SemaphoreType.DMA((3,)),
        ],
        place=[pltpu.HBM] * 3,
    )
    sizes = [1 if step + 1 == rounds or rounds == 2 else 2 for step in range(rounds)] or [2]
    since, peak, level, total, message = call(
        functools.partial(local_body, rounds),
        [((2 * dates, *plane), f32)] + [(plane, f32)] * 3 + [((sizes[0], *plane), f32)],
        keep,
        other,
    )
    (columns_send,) = call(
        functools.partial(halves_body, chips),
        [((dates, paths, width // 2), f32)],
        held,
        message,
        unread=1,
    )
    columns_got = lax.ppermute(columns_send, "date", cores)
    own_level, own_total, state, got = level, total, None, None
    if rounds == 2:
        near = lax.ppermute(message, "date", date_pairs(chips, 1))
        beside = lax.ppermute(total, "date", date_pairs(chips, 1))
        across = lax.ppermute(total, "date", inner_pairs())
        (message,) = call(pair_body, [((1, *plane), f32)], total, message, near)
        far = lax.ppermute(message, "date", date_pairs(chips, 2))
        given, turn = [near, far, beside, across], [beside, across]
        join = lambda *refs: joined_four(*refs[:4])
    else:
        for step in range(rounds):
            got = lax.ppermute(message, "date", date_pairs(chips, 1 << step))
            if step + 1 == rounds:
                break
            body = functools.partial(merge_body, step, rounds)
            if state is None:
                body = lambda a, b, c, *o, body=body: body(a, b, None, c, *o)
            operands = [level, total, got] if state is None else [level, total, state, got]
            group = [(plane, f32)] * (0 if step + 2 == rounds else 2)
            state, message, *group = call(
                body, [((4, *plane), f32), ((sizes[step + 1], *plane), f32)] + group, *operands
            )
            level, total = group or (level, total)
        given, turn = [x for x in (state, got) if x is not None], [message]

        def join(*refs, joined=joined):
            *refs, zero = refs
            held = refs[0] if state is not None else None
            return joined(rounds, held, refs[-1] if got is not None else None, zero)

    (columns,) = call(
        functools.partial(columns_body, chips),
        [((width // 2, 2 * dates * paths), bf16)],
        held,
        columns_got,
        *turn,
        unread=len(turn),
        flops=1 << 27,
    )
    (tail,) = call(
        functools.partial(tail_body, join),
        [((2 * dates * half + STAT_ROWS, contracts), f32)],
        since,
        peak,
        own_level,
        own_total,
        *given,
        columns,
        unread=1,
    )
    tail_other = lax.ppermute(tail, "date", cores)
    steps = count.bit_length() - 1
    assert count == 1 << steps and steps > 0
    near, far = list(range(chips // 2)), list(range(chips // 2, chips))

    def piece(n, part, stats=False):
        return ((n * part * rows + (STAT_ROWS if stats else 0), contracts), f32)

    def over_path(step, message, near=False):
        return lax.ppermute(message, ("date", "path"), path_pairs(chips, count, step, near))

    def next_round(step, given, after, part, stats):
        n = count >> step
        return call(
            functools.partial(path_sum_body, step, not stats),
            [piece(n // 2, part, stats)] * 2,
            *given,
            *after,
            unread=len(after),
            scratch=[pltpu.VMEM((part, n, rows, contracts), f32)],
        )

    (begun,) = call(
        functools.partial(first_body, -1.0 / paths_total),
        [((width // 2, contracts), f32)],
        columns,
        tail,
        flops=dates * paths * width * contracts,
    )
    (message,) = call(
        functools.partial(far_half, -1.0 / paths_total, far, False),
        [piece(count // 2, len(far), True)],
        columns,
        begun,
        tail,
        tail_other,
        scratch=[pltpu.VMEM((count, rows, contracts), f32)],
        flops=dates * paths * width * contracts // 4,
    )
    got = over_path(0, message)
    keep, *firsts = call(
        functools.partial(near_body, -1.0 / paths_total, far, near),
        [piece(count // 2, len(far), True)] + [piece(count, 1)] * len(near),
        columns,
        begun,
        tail,
        tail_other,
        message,
        unread=1,
        scratch=[pltpu.VMEM((count, rows, contracts), f32)],
        flops=3 * dates * paths * width * contracts // 4,
    )
    near_parts = [lax.ppermute(x, "date", date_pairs(chips, j)) if j else x for j, x in zip(near, firsts)]
    assert steps > 1
    for step in range(1, steps):
        keep, message = next_round(step, [keep, got], [], len(far), True)
        got = over_path(step, message)
        near_keep, near_message = next_round(step - 1, near_parts, [message], 1, False)
        near_parts = [near_keep, over_path(step - 1, near_message, True)]
    *sums, stats = call(
        functools.partial(part_sum_body, rows),
        [((2 * rows + STAT_ROWS, contracts // 2), f32)] * len(far) + [((STAT_ROWS, contracts), f32)],
        keep,
        got,
        near_message,
        unread=1,
    )
    over = [lax.ppermute(x, "date", date_pairs(chips, j)) for j, x in zip(far, sums)]
    near_keep, near_message = next_round(steps - 1, near_parts, sums[:1], 1, False)
    over += [near_keep, over_path(steps - 1, near_message, True)]
    gradient, bound, spread = call(
        functools.partial(date_sum_body, chips, len(far), paths_total),
        [((rows, contracts), f32), ((1, contracts), f32), ((1, contracts), f32)],
        stats,
        *over,
    )
    return gradient, bound.reshape(contracts), spread.reshape(contracts)


def solution(mesh):
    placed = (P("date", "path", None), P("date", "path", None), P(), P("date", None))
    return jax.shard_map(
        shards,
        mesh=mesh,
        in_specs=placed,
        out_specs=(P(("date", "path"), None), P(), P()),
        check_vma=False,
    )
```
